128 devices in a mesh: row: 16 (over x_lo, y, core), col: 8 (over z, x_hi).
Axes of the slice: x: 4 (x_hi: 2, x_lo: 2; x = x_hi * 2 + x_lo), y: 4, z: 4, core: 2. Of those that a mesh axis runs over, the one named last changes fastest.
Arguments:
- ortho_in: bfloat16 [7168, 9216], P(('row', 'col')), may hold values from -6 to 6
Outputs:
- next_iterate: bfloat16 [7168, 9216], P(('row', 'col'))
The draws below stay inside these ranges and needn't reach their ends.
All inputs are finite; a program needn't handle non-finite values.
Results may differ from the reference program's by a relative error of at most 0.024.
Values may be sent and summed in bfloat16 or wider, within the bound.
A program may use at most 128 MiB of HBM per device.

```python
import math
import jax
import jax.numpy as jnp
from jax import lax

D = 7168
FF = 9216
TC = 1152


def draw_ortho_in(key, part):
    key = jax.random.fold_in(key, 11)
    noise_key = jax.random.fold_in(key, 0)
    noise = jax.random.normal(noise_key, (D, FF), jnp.float32)
    values = jnp.clip(noise, -6.0, 6.0)
    return values.astype(jnp.bfloat16)


def setup_inputs(seed: int = 0) -> dict:
    key_of = jax.random.split(jax.random.key(seed), 2)
    ortho_in = draw_ortho_in(jax.random.fold_in(key_of[1], 71), 0)
    return dict(ortho_in=ortho_in)


coef_a = 3.4445
coef_b = -4.775
coef_c = 2.0315

def reference(ortho_in):
    ortho_f = ortho_in.astype(jnp.float32)
    inv_square = 1.0 / (math.sqrt(D) + math.sqrt(FF)) ** 2

    def add_block(index, total):
        block = lax.dynamic_slice_in_dim(ortho_f, (index * TC).astype(jnp.int32), TC, 1)
        partial_gram = jnp.dot(block, block.T, precision=lax.Precision.HIGHEST)
        rounded = lax.optimization_barrier(partial_gram.astype(jnp.bfloat16))
        return total + rounded.astype(jnp.float32)
    gram_sum = lax.fori_loop(0, FF // TC, add_block, jnp.zeros((D, D), jnp.float32))
    gram_f = (gram_sum * inv_square).astype(jnp.bfloat16).astype(jnp.float32)
    first_prod = jnp.dot(gram_f, ortho_f, precision=lax.Precision.HIGHEST).astype(jnp.bfloat16)
    second_prod = jnp.dot(gram_f, first_prod.astype(jnp.float32), precision=lax.Precision.HIGHEST)
    iterate = coef_a * ortho_f + coef_b * first_prod.astype(jnp.float32) + coef_c * second_prod
    return iterate.astype(jnp.bfloat16)
```

```python
import functools
import math

import jax
import jax.numpy as jnp
from jax import lax
from jax.experimental import pallas as pl
from jax.experimental.pallas import tpu as pltpu
from jax.sharding import PartitionSpec as P

coef_a = 3.4445
coef_b = -4.775
coef_c = 2.0315

MESH = pl.DeviceIdType.MESH
F32 = jnp.float32
BF16 = jnp.bfloat16

ROWS = 112
HALF = 56
PW = 1152
BLK = 1792
CUT = 512
HB = BLK // 2


def kernel(
    inv_square,
    xin,
    out,
    sb,
    ex,
    stage,
    xp,
    yp,
    pbuf,
    rbuf,
    rx,
    gb,
    zacc,
    oin,
    sem_misc,
    sem_a2a,
    sem_ag,
    sem_agd,
    sem_rs,
    sem_send,
    sem_g,
    sem_back,
):
    row, col = lax.axis_index("row"), lax.axis_index("col")
    k = row % 2
    y = (row // 2) % 4
    x = (col % 2) * 2 + row // 8
    z = col // 2
    r_x = ((x + 1) // 2) % 2
    c_x = x // 2
    rho = r_x * 4 + y

    def dev(xx, yy, zz, kk):
        return (((xx % 2) * 4 + yy) * 2 + kk, zz * 2 + xx // 2)

    x_row = x + 1 - 2 * (x % 2)
    x_col = 3 - x
    ring = {1: dev(x, (y + 1) % 4, z, k), -1: dev(x, (y + 3) % 4, z, k)}
    pair = dev(x_row, y, z, k)
    zring = {1: dev(x, y, (z + 1) % 4, k), -1: dev(x, y, (z + 3) % 4, k)}
    cpair = dev(x_col, y, z, k)
    sib = dev(x, y, z, 1 - k)
    same = k == c_x
    x_far = x + (x_col - x) * (k + c_x - 2 * k * c_x)
    far = [dev(x_far, y, (z + d) % 4, c_x) for d in range(4)]

    def rdma(src, dst, ssem, rsem, device):
        return pltpu.make_async_remote_copy(
            src_ref=src,
            dst_ref=dst,
            send_sem=ssem,
            recv_sem=rsem,
            device_id=device,
            device_id_type=MESH,
        )

    def wait_bytes(ref, sem):
        pltpu.make_async_copy(ref, ref, sem).wait()

    def rows_of(slot):
        return pl.ds(pl.multiple_of(slot * ROWS, 16), ROWS)

    barrier = pltpu.get_barrier_semaphore()
    for d in (ring[1], ring[-1], pair, zring[1], zring[-1], cpair, sib, *far[1:]):
        pl.semaphore_signal(barrier, inc=1, device_id=d, device_id_type=MESH)

    @pl.when(jnp.logical_not(same))
    def _():
        pl.semaphore_signal(barrier, inc=1, device_id=far[0], device_id_type=MESH)

    half = 4 * PW
    mine = pl.ds(pl.multiple_of(k * half, 128), half)
    other = pl.ds(pl.multiple_of((1 - k) * half, 128), half)
    my_rows = pl.ds(pl.multiple_of(k * HALF, 8), HALF)
    other_rows = pl.ds(pl.multiple_of((1 - k) * HALF, 8), HALF)
    sb[...] = xin[:, other].astype(F32)
    ex[my_rows, :] = xin[:, mine].astype(F32)
    pl.semaphore_wait(barrier, 10 + k + c_x - 2 * k * c_x)
    swap = rdma(sb, ex.at[my_rows], sem_misc.at[0], sem_misc.at[1], sib)
    swap.start()
    swap.wait()
    for i in range(4):
        stage[i] = ex[:, i * PW : (i + 1) * PW].astype(BF16)

    my_slot = c_x * 8 + rho
    for d in (0, 1, 3, 2):
        dst = xp.at[z, rows_of(my_slot)]
        if d == 0:

            @pl.when(same)
            def _():
                pltpu.make_async_copy(stage.at[z], dst, sem_a2a.at[z]).start()

            @pl.when(jnp.logical_not(same))
            def _():
                rdma(
                    stage.at[z], dst, sem_send.at[14], sem_a2a.at[z], far[0]
                ).start()

        else:
            rdma(
                stage.at[(z + d) % 4], dst, sem_send.at[14 + d], sem_a2a.at[z], far[d]
            ).start()

    def wait_a2a(u):
        wait_bytes(xp.at[u, rows_of(k * 8 + rho)], sem_a2a.at[u])

    def slot_of(s, e):
        rr = r_x if s == 0 else 1 - r_x
        return k * 8 + rr * 4 + (y + e + 4) % 4

    class Gather:
        def __init__(self, buf, base, t, u):
            self.buf, self.base, self.t, self.u = buf, base, t, u
            self.par = 1 if t % 2 == 0 else -1

        def piece(self, s, e, part="AB"):
            ref = self.buf.at[self.u, rows_of(slot_of(s, e))]
            if part == "A":
                ref = ref.at[:, pl.ds(0, CUT)]
            elif part == "B":
                ref = ref.at[:, pl.ds(CUT, PW - CUT)]
            return ref

        IDX = {
            (0, -1, "AB"): 0,
            (0, 1, "AB"): 1,
            (0, 2, "AB"): 2,
            (1, 0, "AB"): 3,
            (1, -1, "A"): 4,
            (1, -1, "B"): 5,
            (1, 1, "A"): 6,
            (1, 1, "B"): 7,
            (1, 2, "A"): 8,
            (1, 2, "B"): 9,
        }

        def rsem(self, *key):
            return sem_ag.at[self.base * 4 + self.t, self.IDX[key]]

        def send(self, s, e, part, device, key):
            ref = self.piece(s, e, part)
            rdma(
                ref, ref, sem_send.at[self.base * 4 + self.t], self.rsem(*key), device
            ).start()

        def to_sib(self, s, e):
            ref = self.piece(s, e)
            i = self.base * 4 + self.t
            rdma(ref, ref, sem_agd.at[i, 0], sem_agd.at[i, 1], sib).start()

        def wait(self, s, e, part):
            wait_bytes(self.piece(s, e, part), self.rsem(s, e, part))

        def own(self):
            self.send(0, 0, "AB", ring[1], (0, -1, "AB"))
            self.send(0, 0, "AB", ring[-1], (0, 1, "AB"))
            self.send(0, 0, "AB", pair, (1, 0, "AB"))
            self.to_sib(0, 0)

        def level1(self):
            self.wait(1, 0, "AB")
            self.send(1, 0, "B", ring[1], (1, -1, "B"))
            self.send(1, 0, "B", ring[-1], (1, 1, "B"))
            self.to_sib(1, 0)
            for e in (-1, 1):
                self.wait(0, e, "AB")
                if e == -self.par:
                    self.send(0, e, "AB", ring[self.par], (0, 2, "AB"))
                self.send(0, e, "A", pair, (1, e, "A"))
                self.to_sib(0, e)

        def level2(self):
            self.wait(1, -self.par, "B")
            self.send(1, -self.par, "B", ring[self.par], (1, 2, "B"))
            self.wait(0, 2, "AB")
            self.send(0, 2, "A", pair, (1, 2, "A"))
            self.to_sib(0, 2)

        def level3(self):
            self.wait(1, self.par, "B")
            for e in (-1, 1):
                self.wait(1, e, "A")
                self.to_sib(1, e)
            self.wait(1, 2, "B")
            self.wait(1, 2, "A")
            self.to_sib(1, 2)

        def all_here(self):
            i = self.base * 4 + self.t
            ref = self.buf.at[self.u, pl.ds(pl.multiple_of((1 - k) * HB, 16), HB)]
            wait_bytes(ref, sem_agd.at[i, 1])

        def sent(self):
            i = self.base * 4 + self.t
            wait_bytes(self.buf.at[self.u, pl.ds(0, 7 * ROWS)], sem_send.at[i])
            wait_bytes(self.buf.at[self.u, pl.ds(0, HB)], sem_agd.at[i, 0])

    def tile():
        return jnp.concatenate(
            [xp[v, rows_of(k * 8 + rho), :] for v in range(4)], axis=0
        )

    def half_cols(c):
        return pl.ds(c * HB, HB)

    def partial_gram(u, c):
        for n in range(2):
            cols = pl.ds(c * HB + n * 448, 448)
            part = lax.dot_general(
                tile(),
                xp[u, cols, :],
                (((1,), (1,)), ((), ())),
                preferred_element_type=F32,
            ).astype(BF16)
            for v in range(4):
                pbuf[u, v, :, cols] = part[v * ROWS : (v + 1) * ROWS]

    def rs_send(src, dst, u, c, i, device):
        rdma(src, dst, sem_send.at[8 + u], sem_rs.at[u * 2 + c, i], device).start()

    def rs1(u, c):
        s = 1 if c == 0 else -1
        h = half_cols(c)
        rs_send(
            pbuf.at[u, (z + 2) % 4, :, h], rbuf.at[u, 0, :, h], u, c, 0, zring[s]
        )
        rs_send(
            pbuf.at[u, (z + 4 - s) % 4, :, h], rbuf.at[u, 1, :, h], u, c, 1, zring[-s]
        )

    def rs2(u, c):
        s = 1 if c == 0 else -1
        h = half_cols(c)
        v = (z + 4 + s) % 4
        wait_bytes(rbuf.at[u, 0, :, h], sem_rs.at[u * 2 + c, 0])
        pbuf[u, v, :, h] = (
            pbuf[u, v, :, h].astype(F32) + rbuf[u, 0, :, h].astype(F32)
        ).astype(BF16)
        rs_send(pbuf.at[u, v, :, h], rbuf.at[u, 2, :, h], u, c, 2, zring[s])

    def rs3(u, c):
        h = half_cols(c)
        wait_bytes(rbuf.at[u, 1, :, h], sem_rs.at[u * 2 + c, 1])
        wait_bytes(rbuf.at[u, 2, :, h], sem_rs.at[u * 2 + c, 2])
        pbuf[u, z, :, h] = (
            pbuf[u, z, :, h].astype(F32)
            + rbuf[u, 1, :, h].astype(F32)
            + rbuf[u, 2, :, h].astype(F32)
        ).astype(BF16)
        rs_send(pbuf.at[u, z, :, h], rx.at[u, :, h], u, c, 3, cpair)

    def rs4(u, c):
        h = half_cols(c)
        wait_bytes(rx.at[u, :, h], sem_rs.at[u * 2 + c, 3])
        total = pbuf[u, z, :, h].astype(F32) + rx[u, :, h].astype(F32)
        gb[z, u, :, h] = (total * inv_square).astype(BF16)

    ax = [Gather(xp, 0, u, u) for u in range(4)]
    wait_a2a(0)
    ax[0].own()
    for u in range(4):
        ax[u].level1()
        if u == 0:
            wait_a2a(1)
        if u < 3:
            ax[u + 1].own()
        if u > 0:
            rs2(u - 1, 0)
            rs2(u - 1, 1)
        ax[u].level2()
        if u > 0:
            rs3(u - 1, 0)
            rs3(u - 1, 1)
        ax[u].level3()
        if u == 0:
            wait_a2a(2)
            wait_a2a(3)
        if u > 0:
            rs4(u - 1, 0)
            rs4(u - 1, 1)
        ax[u].all_here()
        for c in range(2):
            partial_gram(u, c)
            rs1(u, c)
    for f in (rs2, rs3, rs4):
        for c in range(2):
            f(3, c)

    def u_of(w):
        return w + c_x * (3 - 2 * w)

    def gref(e, w, h=None):
        ref = gb.at[(z + e + 4) % 4, u_of(w)]
        return ref if h is None else ref.at[:, half_cols(h)]

    def g_send(e, w, device, i, h=None):
        rdma(gref(e, w, h), gref(e, w, h), sem_send.at[12], sem_g.at[i], device).start()

    def g_wait(e, w, i, h=None):
        wait_bytes(gref(e, w, h), sem_g.at[i])

    for w in range(3):
        g_send(0, w, zring[1], w)
        g_send(0, w, zring[-1], 3 + w)

    ay = [Gather(yp, 1, t, (z + e) % 4) for t, e in enumerate((0, 3, 1, 2))]

    def first_prod(t):
        v = ay[t].u
        acc = jnp.dot(gb[v, 0], xp[0], preferred_element_type=F32)
        zacc[pl.ds(0, ROWS), :] = acc
        for u in range(1, 4):
            zacc[pl.ds(0, ROWS), :] += jnp.dot(
                gb[v, u], xp[u], preferred_element_type=F32
            )
        yp[v, rows_of(k * 8 + rho), :] = zacc[pl.ds(0, ROWS), :].astype(BF16)

    def second_prod(t):
        v = ay[t].u
        g = jnp.concatenate([gb[i, v] for i in range(4)], axis=0)
        for n in range(3):
            cols = pl.ds(n * 384, 384)
            term = jnp.dot(g, yp[v, :, cols], preferred_element_type=F32)
            if t == 0:
                zacc[:, cols] = term
            else:
                zacc[:, cols] += term

    first_prod(0)
    ay[0].own()

    g_wait(-1, 0, 0)
    g_send(-1, 0, cpair, 10)
    g_send(-1, 0, zring[1], 6)
    g_wait(1, 0, 3)
    g_send(1, 0, cpair, 11)
    ay[0].level1()
    g_wait(-1, 1, 1)
    g_wait(1, 1, 4)
    g_send(1, 1, zring[-1], 7)
    ay[0].level2()
    ay[0].level3()
    g_wait(-1, 2, 2)
    g_send(-1, 2, zring[1], 8, 0)
    g_wait(1, 2, 5)
    g_send(1, 2, zring[-1], 9, 1)
    g_wait(-1, 3, 10)
    first_prod(1)
    ay[1].own()
    g_wait(1, 3, 11)
    first_prod(2)
    ay[1].level1()
    ay[2].own()
    g_wait(2, 0, 6)
    g_send(2, 0, cpair, 12)
    ay[1].level2()
    ay[2].level1()
    g_wait(2, 1, 7)
    g_wait(2, 2, 8, 0)
    g_wait(2, 2, 9, 1)
    g_wait(2, 3, 12)
    first_prod(3)
    ay[3].own()
    ay[1].level3()
    ay[2].level2()
    ay[0].all_here()
    second_prod(0)
    ay[3].level1()
    ay[2].level3()
    ay[1].all_here()
    second_prod(1)
    ay[3].level2()
    ay[2].all_here()
    second_prod(2)
    ay[3].level3()
    ay[3].all_here()
    second_prod(3)

    for d in range(4):
        wait_bytes(stage.at[(z + d) % 4], sem_send.at[14 + d]) if d else None

    @pl.when(jnp.logical_not(same))
    def _():
        wait_bytes(stage.at[z], sem_send.at[14])

    for v in range(4):
        own = rows_of(k * 8 + rho)
        it = (
            coef_a * xp[v, own, :].astype(F32)
            + coef_b * yp[v, own, :].astype(F32)
            + coef_c * zacc[pl.ds(v * ROWS, ROWS), :]
        )
        stage[v] = it.astype(BF16)
    for d in (2, 1, 3, 0):
        src, dst = stage.at[(z + d) % 4], oin.at[z]
        if d == 0:

            @pl.when(same)
            def _():
                pltpu.make_async_copy(src, dst, sem_back.at[z]).start()

            @pl.when(jnp.logical_not(same))
            def _():
                rdma(src, dst, sem_send.at[18], sem_back.at[z], far[0]).start()

        else:
            rdma(src, dst, sem_send.at[18 + d], sem_back.at[z], far[d]).start()
    for v in range(4):
        wait_bytes(oin.at[v], sem_back.at[v])
    for v in range(4):
        ex[:, v * PW : (v + 1) * PW] = oin[v].astype(F32)
    back = rdma(ex.at[other_rows], sb, sem_misc.at[2], sem_misc.at[3], sib)
    back.start()
    out[:, mine] = ex[my_rows, :].astype(BF16)
    back.wait()
    out[:, other] = sb[...].astype(BF16)

    for g in (*ax, *ay):
        g.sent()
    for u in range(4):
        wait_bytes(pbuf.at[u], sem_send.at[8 + u])
    wait_bytes(gb.at[pl.ds(0, 3)], sem_send.at[12])
    for d in range(1, 4):
        wait_bytes(stage.at[(z + d) % 4], sem_send.at[18 + d])

    @pl.when(jnp.logical_not(same))
    def _():
        wait_bytes(stage.at[z], sem_send.at[18])


def solution(mesh):
    def step(ortho_in):
        rows, full_cols = ortho_in.shape
        full_rows = rows * mesh.size
        inv_square = 1.0 / (math.sqrt(full_rows) + math.sqrt(full_cols)) ** 2
        vmem = pltpu.VMEM
        dma = pltpu.SemaphoreType.DMA
        return pl.pallas_call(
            functools.partial(kernel, inv_square),
            name="newton_schulz",
            out_shape=jax.ShapeDtypeStruct((rows, full_cols), BF16),
            in_specs=[pl.BlockSpec(memory_space=pltpu.VMEM)],
            out_specs=pl.BlockSpec(memory_space=pltpu.VMEM),
            scratch_shapes=[
                vmem((HALF, 4 * PW), F32),
                vmem((ROWS, 4 * PW), F32),
                vmem((4, ROWS, PW), BF16),
                vmem((4, BLK, PW), BF16),
                vmem((4, BLK, PW), BF16),
                vmem((4, 4, ROWS, BLK), BF16),
                vmem((4, 3, ROWS, BLK), BF16),
                vmem((4, ROWS, BLK), BF16),
                vmem((4, 4, ROWS, BLK), BF16),
                vmem((4 * ROWS, PW), F32),
                vmem((4, ROWS, PW), BF16),
                dma((4,)),
                dma((4,)),
                dma((8, 10)),
                dma((8, 2)),
                dma((8, 4)),
                dma((22,)),
                dma((13,)),
                dma((4,)),
            ],
            compiler_params=pltpu.CompilerParams(
                collective_id=0,
                has_side_effects=True,
                vmem_limit_bytes=64 * 2**20 - 2**18,
            ),
            cost_estimate=pl.CostEstimate(
                flops=3 * 2 * 448 * 7168 * 1152,
                bytes_accessed=4 * 56 * 9216,
                transcendentals=0,
            ),
        )(ortho_in)

    spec = P(("row", "col"), None)
    return jax.shard_map(
        step, mesh=mesh, in_specs=(spec,), out_specs=spec, check_vma=False
    )
```

```python
import functools
import math

import jax
import jax.numpy as jnp
from jax import lax
from jax.experimental import pallas as pl
from jax.experimental.pallas import tpu as pltpu
from jax.sharding import PartitionSpec as P

coef_a = 3.4445
coef_b = -4.775
coef_c = 2.0315

MESH = pl.DeviceIdType.MESH
F32 = jnp.float32
BF16 = jnp.bfloat16

ROWS = 112
HALF = 56
PAD = 64
PW = 1152
BLK = 1792
HB = BLK // 2
SIDE = 4 * ROWS
X_PASS = (0, PW, 512)
Y_PASS = ((0, 640, 256), (640, 512, 256))

ORDER = (
    "a0", "x0o", "a1", "x1o", "a2", "a3", "x0m", "x0q", "x0p", "x1m", "x1q", "x1p", "x0r", "x0b",
    "x1r", "x2o", "g00", "x1b", "g10", "x0e", "s00", "x2q", "g01", "x2m", "x1e", "x3o", "s10",
    "x2p", "g11", "t00", "s01", "x2r", "x3q", "x3p", "g20", "w00", "s11", "x3m", "t10", "t01",
    "x2b", "x3r", "x3b", "g30", "w10", "x2e", "s20", "t11", "w01", "x3e", "g21", "s30", "g31",
    "w11", "t20", "s21", "s31", "w20", "t30", "t21", "t31", "h0", "w30", "w21", "h2", "w31", "h3",
    "f0", "i0", "j0", "y10o", "y00o", "y10m", "y10p", "y10q", "i2", "j2", "y00m", "y00q", "y00p",
    "y10r", "y10b", "y00r", "i3", "j3", "f1", "y00b", "y11o", "y10e", "y01o", "f2", "k0", "y00e",
    "y12o", "y11p", "y11q", "y02o", "y11m", "y01q", "y01p", "y01m", "y12q", "y12p", "y11b", "y12m",
    "y11r", "f3", "z10", "z00", "y01r", "y12b", "y02q", "y02m", "y02p", "y13o", "y12r", "y01b",
    "y03o", "y11e", "y02r", "z11", "y13p", "y02b", "y13q", "y12e", "y01e", "y13m", "z12", "z01",
    "y13b", "y03q", "y03m", "y03p", "y02e", "y13r", "z02", "y13e", "y03r", "y03b", "z13", "o1",
    "y03e", "z03", "o0", "v1", "v0",
)


def kernel(
    inv_square,
    xin,
    out,
    xs,
    ain,
    xp,
    yp,
    pbuf,
    rbuf,
    rx,
    gb,
    zacc,
    fin,
    oin,
    sem_a2a,
    sem_ag,
    sem_agd,
    sem_rs,
    sem_g,
    sem_back,
    sem_send,
):
    row, col = lax.axis_index("row"), lax.axis_index("col")
    k = row % 2
    y = (row // 2) % 4
    x = (col % 2) * 2 + row // 8
    z = col // 2
    r_x = ((x + 1) // 2) % 2
    c_x = x // 2

    def dev(xx, yy, zz, kk):
        return (((xx % 2) * 4 + yy) * 2 + kk, zz * 2 + xx // 2)

    x_row = x + 1 - 2 * (x % 2)
    x_col = 3 - x
    ring = {1: dev(x, (y + 1) % 4, z, k), -1: dev(x, (y + 3) % 4, z, k)}
    pair = dev(x_row, y, z, k)
    zring = {1: dev(x, y, (z + 1) % 4, k), -1: dev(x, y, (z + 3) % 4, k)}
    cpair = dev(x_col, y, z, k)
    sib = dev(x, y, z, 1 - k)
    same = k == c_x
    other = k + c_x - 2 * k * c_x
    x_far = x + (x_col - x) * other

    def rdma(src, dst, ssem, rsem, device):
        return pltpu.make_async_remote_copy(
            src_ref=src,
            dst_ref=dst,
            send_sem=ssem,
            recv_sem=rsem,
            device_id=device,
            device_id_type=MESH,
        )

    def wait_bytes(ref, sem):
        pltpu.make_async_copy(ref, ref, sem).wait()

    def rows_at(start, n):
        return pl.ds(pl.multiple_of(start, 16), n)

    def cols_at(start, n):
        return pl.ds(pl.multiple_of(start, 128), n)

    def move(src, dst, ssem, rsem, device, self_too):
        if not self_too:
            rdma(src, dst, ssem, rsem, device).start()
            return

        @pl.when(same)
        def _():
            pltpu.make_async_copy(src, dst, rsem).start()

        @pl.when(jnp.logical_not(same))
        def _():
            rdma(src, dst, ssem, rsem, device).start()

    barrier = pltpu.get_barrier_semaphore()

    def greet(device):
        pl.semaphore_signal(barrier, inc=1, device_id=device, device_id_type=MESH)

    way_in = []
    for d in (0, 1, 3, 2):
        for i in range(2):
            xx, cc = (x, c_x) if i == 0 else (x_col, 1 - c_x)
            zz = (z + d) % 4
            way_in.append((dev(xx, y, zz, c_x), cc, zz, d == 0 and i == 0))
    way_back = []
    for d in (2, 1, 3, 0):
        for i in range(2):
            kk = k if i == 0 else 1 - k
            zz = (z + d) % 4
            way_back.append((dev(x_far, y, zz, kk), zz, kk, d == 0 and i == 0))
    for d in (ring[1], ring[-1], pair, zring[1], zring[-1], cpair, sib):
        greet(d)
    for d, _, _, self_too in way_in + way_back:
        if not self_too:
            greet(d)

    @pl.when(jnp.logical_not(same))
    def _():
        for d, _, _, self_too in way_in + way_back:
            if self_too:
                greet(d)

    xs[...] = jnp.concatenate(
        [xin[...].astype(F32), jnp.zeros((PAD - HALF, 8 * PW), F32)], axis=0
    ).astype(BF16)
    pl.semaphore_wait(barrier, 21 + 2 * other)

    for device, cc, zz, self_too in way_in:
        move(
            xs.at[:, cols_at((cc * 4 + zz) * PW, PW)],
            ain.at[rows_at((z * 2 + k) * PAD, PAD)],
            sem_send.at[0, 1 if self_too else 0],
            sem_a2a.at[z * 2 + k],
            device,
            self_too,
        )

    my_slot = (r_x * 2 + k) * 4 + y
    my_rows = rows_at(my_slot * ROWS, ROWS)

    def assemble(u):
        parts = []
        for kk in range(2):
            ref = ain.at[pl.ds((u * 2 + kk) * PAD, PAD)]
            wait_bytes(ref, sem_a2a.at[u * 2 + kk])
            parts.append(ref[...].astype(F32)[:HALF])
        xp[u, my_rows, :] = jnp.concatenate(parts, axis=0).astype(BF16)

    class Gather:
        IDX = {
            (0, -1, "AB"): 0,
            (0, 1, "AB"): 1,
            (0, 2, "AB"): 2,
            (1, 0, "AB"): 3,
            (1, -1, "A"): 4,
            (1, -1, "B"): 5,
            (1, 1, "A"): 6,
            (1, 1, "B"): 7,
            (1, 2, "A"): 8,
            (1, 2, "B"): 9,
        }

        def __init__(self, buf, i, par, u, cols):
            self.buf, self.i, self.u = buf, i, u
            self.par = par
            self.start, self.width, self.cut = cols

        def area(self, rows):
            return self.buf.at[self.u, rows, pl.ds(self.start, self.width)]

        def piece(self, s, e, part="AB"):
            rr = r_x if s == 0 else 1 - r_x
            slot = (rr * 2 + k) * 4 + (y + e + 4) % 4
            cols = pl.ds(self.start, self.width)
            if part == "A":
                cols = pl.ds(self.start, self.cut)
            elif part == "B":
                cols = pl.ds(self.start + self.cut, self.width - self.cut)
            return self.buf.at[self.u, rows_at(slot * ROWS, ROWS), cols]

        def rsem(self, *key):
            return sem_ag.at[self.i, self.IDX[key]]

        def send(self, s, e, part, device, key):
            ref = self.piece(s, e, part)
            rdma(ref, ref, sem_agd.at[self.i, 0], self.rsem(*key), device).start()

        def side(self, s, kk):
            rr = r_x if s == 0 else 1 - r_x
            return self.area(rows_at((rr * 2 + kk) * SIDE, SIDE))

        def to_sib(self, s):
            ref = self.side(s, k)
            rdma(
                ref, ref, sem_agd.at[self.i, 1], sem_agd.at[self.i, 2 + s], sib
            ).start()

        def wait(self, s, e, part):
            wait_bytes(self.piece(s, e, part), self.rsem(s, e, part))

        def o(self):
            self.send(0, 0, "AB", ring[1], (0, -1, "AB"))
            self.send(0, 0, "AB", ring[-1], (0, 1, "AB"))
            self.send(0, 0, "AB", pair, (1, 0, "AB"))

        def p(self):
            self.wait(1, 0, "AB")
            for s in (self.par, -self.par):
                self.send(1, 0, "B", ring[s], (1, -s, "B"))

        def first(self, e):
            self.wait(0, e, "AB")
            if e == -self.par:
                self.send(0, e, "AB", ring[self.par], (0, 2, "AB"))
            self.send(0, e, "A", pair, (1, e, "A"))

        def m(self):
            self.first(-1)

        def q(self):
            self.first(1)

        def b(self):
            self.wait(1, -self.par, "B")
            self.send(1, -self.par, "B", ring[self.par], (1, 2, "B"))

        def r(self):
            self.wait(0, 2, "AB")
            self.send(0, 2, "A", pair, (1, 2, "A"))
            self.to_sib(0)

        def e(self):
            self.wait(1, self.par, "B")
            for e in (-1, 1):
                self.wait(1, e, "A")
            self.wait(1, 2, "B")
            self.wait(1, 2, "A")
            self.to_sib(1)

        def here(self, s):
            wait_bytes(self.side(s, 1 - k), sem_agd.at[self.i, 2 + s])

        def sent(self):
            wait_bytes(self.area(pl.ds(0, 7 * ROWS)), sem_agd.at[self.i, 0])
            wait_bytes(self.area(pl.ds(0, 2 * SIDE)), sem_agd.at[self.i, 1])

    ax = [Gather(xp, u, 1 - 2 * (u % 2), u, X_PASS) for u in range(4)]
    steps = [z, (z + 3) % 4, (z + 1) % 4, (z + 2) % 4]
    ay = [
        [
            Gather(yp, 4 + 4 * n + t, 1 - 2 * (t % 2), steps[t], cols)
            for t in range(4)
        ]
        for n, cols in enumerate(Y_PASS)
    ]

    def side_start(c):
        return (r_x if c == 0 else 1 - r_x) * HB

    def side_cols(c):
        return cols_at(side_start(c), HB)

    def partial_gram(u, c):
        ax[u].here(c)
        tile = jnp.concatenate([xp[v, my_rows, :] for v in range(4)], axis=0)
        for start, n in ((0, 512), (512, 384)):
            part = lax.dot_general(
                tile,
                xp[u, rows_at(side_start(c) + start, n), :],
                (((1,), (1,)), ((), ())),
                preferred_element_type=F32,
            ).astype(BF16)
            cols = cols_at(side_start(c) + start, n)
            for v in range(4):
                pbuf[u, v, :, cols] = part[v * ROWS : (v + 1) * ROWS]
        s = 1 if c == 0 else -1
        h = side_cols(c)
        rs_send(pbuf.at[u, (z + 2) % 4, :, h], rbuf.at[u, 0, :, h], u, c, 0, zring[s])
        rs_send(
            pbuf.at[u, (z + 4 - s) % 4, :, h], rbuf.at[u, 1, :, h], u, c, 1, zring[-s]
        )

    def rs_send(src, dst, u, c, i, device):
        rdma(src, dst, sem_send.at[1, u], sem_rs.at[u * 2 + c, i], device).start()

    def rs_mid(u, c):
        s = 1 if c == 0 else -1
        h = side_cols(c)
        v = (z + 4 + s) % 4
        wait_bytes(rbuf.at[u, 0, :, h], sem_rs.at[u * 2 + c, 0])
        pbuf[u, v, :, h] = (
            pbuf[u, v, :, h].astype(F32) + rbuf[u, 0, :, h].astype(F32)
        ).astype(BF16)
        rs_send(pbuf.at[u, v, :, h], rbuf.at[u, 2, :, h], u, c, 2, zring[s])

    def rs_sum(u, c):
        h = side_cols(c)
        wait_bytes(rbuf.at[u, 1, :, h], sem_rs.at[u * 2 + c, 1])
        wait_bytes(rbuf.at[u, 2, :, h], sem_rs.at[u * 2 + c, 2])
        pbuf[u, z, :, h] = (
            pbuf[u, z, :, h].astype(F32)
            + rbuf[u, 1, :, h].astype(F32)
            + rbuf[u, 2, :, h].astype(F32)
        ).astype(BF16)
        rs_send(pbuf.at[u, z, :, h], rx.at[u, :, h], u, c, 3, cpair)

    def rs_end(u, c):
        h = side_cols(c)
        wait_bytes(rx.at[u, :, h], sem_rs.at[u * 2 + c, 3])
        total = pbuf[u, z, :, h].astype(F32) + rx[u, :, h].astype(F32)
        gb[z, u, :, h] = (total * inv_square).astype(BF16)

    def g_u(j):
        return c_x if j == 0 else j

    def gref(e, u, half=None):
        ref = gb.at[(z + e + 4) % 4, u]
        return ref if half is None else ref.at[:, pl.ds(half * HB, HB)]

    def g_send(ref, device, i):
        rdma(ref, ref, sem_send.at[2, 0], sem_g.at[i], device).start()

    def g_own(j):
        g_send(gref(0, g_u(j)), zring[1], 4 * j)
        g_send(gref(0, g_u(j)), zring[-1], 4 * j + 1)

    def g_pass(j, e):
        u = g_u(j)
        wait_bytes(gref(e, u), sem_g.at[4 * j + (0 if e == -1 else 1)])
        half = 0 if e == -1 else 1
        g_send(gref(e, u, half), zring[-e], 4 * j + 2 + half)
        if j == 0:
            g_send(gref(e, u), cpair, 16 + half)

    def g_far(j):
        for half in range(2):
            wait_bytes(gref(2, g_u(j), half), sem_g.at[4 * j + 2 + half])

    def g_far_pair():
        g_far(0)
        g_send(gref(2, g_u(0)), cpair, 18)

    def g_pair(e):
        wait_bytes(gref(e, 1 - c_x), sem_g.at[16 + (-1, 1, 2).index(e)])

    def first_prod(t):
        if t > 0:
            g_pair((0, -1, 1, 2)[t])
        if t == 3:
            g_far(2)
            g_far(3)
        v = steps[t]
        acc = zacc.at[pl.ds(0, ROWS)]
        acc[...] = jnp.dot(gb[v, 0], xp[0], preferred_element_type=F32)
        for u in range(1, 3):
            acc[...] += jnp.dot(gb[v, u], xp[u], preferred_element_type=F32)
        yp[v, my_rows, :] = (
            acc[...] + jnp.dot(gb[v, 3], xp[3], preferred_element_type=F32)
        ).astype(BF16)

    def second_prod(n, t):
        ay[n][t].here(0)
        ay[n][t].here(1)
        v = steps[t]
        cols = pl.ds(Y_PASS[n][0], Y_PASS[n][1])
        g = jnp.concatenate([gb[i, v] for i in range(4)], axis=0)
        term = jnp.dot(g, yp[v, :, cols], preferred_element_type=F32)
        if t == 0:
            zacc[:, cols] = term
        else:
            zacc[:, cols] += term

    def combine(n):
        cols = pl.ds(Y_PASS[n][0], Y_PASS[n][1])
        gap = jnp.zeros((PAD - HALF, Y_PASS[n][1]), F32)
        for v in range(4):
            it = (
                coef_a * xp[v, my_rows, cols].astype(F32)
                + coef_b * yp[v, my_rows, cols].astype(F32)
                + coef_c * zacc[pl.ds(v * ROWS, ROWS), cols]
            )
            for kk in range(2):
                fin[pl.ds((v * 2 + kk) * PAD, PAD), cols] = jnp.concatenate(
                    [it[kk * HALF : (kk + 1) * HALF], gap], axis=0
                ).astype(BF16)
        for device, zz, kk, self_too in way_back:
            move(
                fin.at[rows_at((zz * 2 + kk) * PAD, PAD), cols],
                oin.at[rows_at((c_x * 4 + z) * PAD, PAD), cols],
                sem_send.at[3 + n, 1 if self_too else 0],
                sem_back.at[n, c_x * 4 + z],
                device,
                self_too,
            )

    def collect(n):
        start, width, _ = Y_PASS[n]
        for g in range(8):
            ref = oin.at[pl.ds(g * PAD, PAD), pl.ds(start, width)]
            wait_bytes(ref, sem_back.at[n, g])
            out[:, pl.ds(g * PW + start, width)] = (
                ref[...].astype(F32)[:HALF].astype(BF16)
            )

    for name in ORDER:
        kind, args = name[0], [int(i) for i in name[1:] if i.isdigit()]
        if kind == "x":
            getattr(ax[args[0]], name[-1])()
        elif kind == "y":
            getattr(ay[args[0]][args[1]], name[-1])()
        elif kind in "ij":
            g_pass(args[0], -1 if kind == "i" else 1)
        else:
            {
                "a": assemble,
                "g": partial_gram,
                "s": rs_mid,
                "t": rs_sum,
                "w": rs_end,
                "h": g_own,
                "k": lambda _: g_far_pair(),
                "f": first_prod,
                "z": second_prod,
                "o": combine,
                "v": collect,
            }[kind](*args)

    for g in (*ax, *(g for n in ay for g in n)):
        g.sent()
    for u in range(4):
        wait_bytes(pbuf.at[u], sem_send.at[1, u])
    wait_bytes(gb.at[pl.ds(0, 3)], sem_send.at[2, 0])
    wait_bytes(ain.at[pl.ds(0, 7 * PAD)], sem_send.at[0, 0])
    for n, (start, width, _) in enumerate(Y_PASS):
        wait_bytes(
            fin.at[pl.ds(0, 7 * PAD), pl.ds(start, width)], sem_send.at[3 + n, 0]
        )

    @pl.when(jnp.logical_not(same))
    def _():
        wait_bytes(ain.at[pl.ds(0, PAD)], sem_send.at[0, 1])
        for n, (start, width, _) in enumerate(Y_PASS):
            wait_bytes(
                fin.at[pl.ds(0, PAD), pl.ds(start, width)], sem_send.at[3 + n, 1]
            )


def solution(mesh):
    def step(ortho_in):
        rows, full_cols = ortho_in.shape
        full_rows = rows * mesh.size
        inv_square = 1.0 / (math.sqrt(full_rows) + math.sqrt(full_cols)) ** 2
        vmem = pltpu.VMEM
        dma = pltpu.SemaphoreType.DMA
        n = len(Y_PASS)
        return pl.pallas_call(
            functools.partial(kernel, inv_square),
            name="newton_schulz",
            out_shape=jax.ShapeDtypeStruct((rows, full_cols), BF16),
            in_specs=[pl.BlockSpec(memory_space=pltpu.VMEM)],
            out_specs=pl.BlockSpec(memory_space=pltpu.VMEM),
            scratch_shapes=[
                vmem((PAD, 8 * PW), BF16),
                vmem((8 * PAD, PW), BF16),
                vmem((4, BLK, PW), BF16),
                vmem((4, BLK, PW), BF16),
                vmem((4, 4, ROWS, BLK), BF16),
                vmem((4, 3, ROWS, BLK), BF16),
                vmem((4, ROWS, BLK), BF16),
                vmem((4, 4, ROWS, BLK), BF16),
                vmem((4 * ROWS, PW), F32),
                vmem((8 * PAD, PW), BF16),
                vmem((8 * PAD, PW), BF16),
                dma((8,)),
                dma((4 + 4 * n, 10)),
                dma((4 + 4 * n, 4)),
                dma((8, 4)),
                dma((19,)),
                dma((n, 8)),
                dma((3 + n, 4)),
            ],
            compiler_params=pltpu.CompilerParams(
                collective_id=0,
                has_side_effects=True,
                vmem_limit_bytes=64 * 2**20 - 2**18,
            ),
            cost_estimate=pl.CostEstimate(
                flops=3 * 2 * 448 * 7168 * 1152,
                bytes_accessed=4 * 56 * 9216,
                transcendentals=0,
            ),
        )(ortho_in)

    spec = P(("row", "col"), None)
    return jax.shard_map(
        step, mesh=mesh, in_specs=(spec,), out_specs=spec, check_vma=False
    )
```

```python
import functools
import math

import jax
import jax.numpy as jnp
from jax import lax
from jax.experimental import pallas as pl
from jax.experimental.pallas import tpu as pltpu
from jax.sharding import PartitionSpec as P

coef_a = 3.4445
coef_b = -4.775
coef_c = 2.0315

MESH = pl.DeviceIdType.MESH
F32 = jnp.float32
BF16 = jnp.bfloat16

ROWS = 112
HALF = 56
PAD = 64
PW = 1152
BLK = 1792
HB = BLK // 2
SIDE = 4 * ROWS
X_PASS = (0, PW, 512)
Y_PASS = ((0, 640, 256), (640, 512, 256))

ORDER = (
    "a0", "x0o", "a1", "x1o", "a2", "a3", "x0m", "x0q", "x0p", "x1m", "x1q", "x1p", "x2o", "x0r",
    "x0b", "x1r", "g00", "g01", "x1b", "g10", "g11", "s00", "x2p", "s01", "x2m", "x2q", "x3o",
    "s10", "x0e", "x1e", "s11", "t01", "t00", "x2b", "g02", "g03", "t11", "t10", "g12", "w01",
    "g13", "w00", "s02", "x2r", "x3q", "w11", "s03", "x3p", "g20", "s12", "w10", "g21", "x3m",
    "s13", "x3r", "t03", "t02", "x2e", "s20", "x3b", "g30", "w03", "g31", "g22", "t12", "t13",
    "w02", "g23", "s21", "x3e", "t20", "w12", "s30", "g32", "s31", "w13", "g33", "s22", "w20",
    "s23", "t21", "t30", "s32", "w21", "t31", "s33", "w30", "t23", "w31", "h0", "t22", "t33", "t32",
    "w23", "w22", "h2", "w33", "w32", "h3", "i0", "f0", "j0", "y00o", "y10o", "y00m", "i2", "y00p",
    "y00q", "j2", "y10m", "y10q", "y10p", "y00r", "y00b", "i3", "f1", "j3", "y01o", "y10b", "y10r",
    "y11o", "y00e", "f2", "k0", "y02o", "y12o", "y01m", "y01q", "y01p", "y10e", "y11q", "y11m",
    "y11p", "y02q", "y02m", "y02p", "y12q", "y12m", "y12p", "f3", "y01r", "z10", "y01b", "y13o",
    "z00", "y11r", "y02r", "y11b", "y03o", "y02b", "y12r", "y12b", "y01e", "y13p", "y13m", "y13q",
    "z01", "y11e", "y03m", "y02e", "y03p", "z11", "y12e", "y13b", "y03q", "z02", "y13r", "z12",
    "y03b", "y13e", "y03r", "z13", "o1", "y03e", "z03", "o0", "v1", "v0",
)


def kernel(
    inv_square,
    xin,
    out,
    xv,
    xs,
    ain,
    xp,
    yp,
    pbuf,
    rbuf,
    rx,
    gb,
    zacc,
    fin,
    sem_in,
    sem_a2a,
    sem_ag,
    sem_agd,
    sem_rs,
    sem_g,
    sem_back,
    sem_send,
):
    row, col = lax.axis_index("row"), lax.axis_index("col")
    k = row % 2
    y = (row // 2) % 4
    x = (col % 2) * 2 + row // 8
    z = col // 2
    r_x = ((x + 1) // 2) % 2
    c_x = x // 2

    def dev(xx, yy, zz, kk):
        return (((xx % 2) * 4 + yy) * 2 + kk, zz * 2 + xx // 2)

    x_row = x + 1 - 2 * (x % 2)
    x_col = 3 - x
    ring = {1: dev(x, (y + 1) % 4, z, k), -1: dev(x, (y + 3) % 4, z, k)}
    pair = dev(x_row, y, z, k)
    zring = {1: dev(x, y, (z + 1) % 4, k), -1: dev(x, y, (z + 3) % 4, k)}
    cpair = dev(x_col, y, z, k)
    sib = dev(x, y, z, 1 - k)
    same = k == c_x
    other = k + c_x - 2 * k * c_x
    x_far = x + (x_col - x) * other

    def rdma(src, dst, ssem, rsem, device):
        return pltpu.make_async_remote_copy(
            src_ref=src,
            dst_ref=dst,
            send_sem=ssem,
            recv_sem=rsem,
            device_id=device,
            device_id_type=MESH,
        )

    def wait_bytes(ref, sem):
        pltpu.make_async_copy(ref, ref, sem).wait()

    def rows_at(start, n):
        return pl.ds(pl.multiple_of(start, 16), n)

    def cols_at(start, n):
        return pl.ds(pl.multiple_of(start, 128), n)

    def move(src, dst, ssem, rsem, device, self_too):
        if not self_too:
            rdma(src, dst, ssem, rsem, device).start()
            return

        @pl.when(same)
        def _():
            pltpu.make_async_copy(src, dst, rsem).start()

        @pl.when(jnp.logical_not(same))
        def _():
            rdma(src, dst, ssem, rsem, device).start()

    load = pltpu.make_async_copy(xin, xv, sem_in.at[0])
    load.start()

    barrier = pltpu.get_barrier_semaphore()

    def greet(device):
        pl.semaphore_signal(barrier, inc=1, device_id=device, device_id_type=MESH)

    way_in = []
    for d in (0, 1, 3, 2):
        for i in range(2):
            xx, cc = (x, c_x) if i == 0 else (x_col, 1 - c_x)
            zz = (z + d) % 4
            way_in.append((dev(xx, y, zz, c_x), cc, zz, d == 0 and i == 0))
    way_back = []
    for d in (2, 1, 3, 0):
        for i in range(2):
            kk = k if i == 0 else 1 - k
            zz = (z + d) % 4
            way_back.append((dev(x_far, y, zz, kk), zz, kk, d == 0 and i == 0))
    for d in (ring[1], ring[-1], pair, sib):
        greet(d)
    for d, _, _, self_too in way_back:
        if not self_too:
            greet(d)
    back_self = way_back[-2][0]

    @pl.when(jnp.logical_not(same))
    def _():
        greet(back_self)

    load.wait()
    xs[...] = jnp.concatenate(
        [xv[...].astype(F32), jnp.zeros((PAD - HALF, 8 * PW), F32)], axis=0
    ).astype(BF16)
    pl.semaphore_wait(barrier, 11 + other)

    for device, cc, zz, self_too in way_in:
        move(
            xs.at[:, cols_at((cc * 4 + zz) * PW, PW)],
            ain.at[rows_at((z * 2 + k) * PAD, PAD)],
            sem_send.at[0, 1 if self_too else 0],
            sem_a2a.at[z * 2 + k],
            device,
            self_too,
        )

    my_slot = (r_x * 2 + k) * 4 + y
    my_rows = rows_at(my_slot * ROWS, ROWS)

    def assemble(u):
        parts = []
        for kk in range(2):
            ref = ain.at[pl.ds((u * 2 + kk) * PAD, PAD)]
            wait_bytes(ref, sem_a2a.at[u * 2 + kk])
            parts.append(ref[...].astype(F32)[:HALF])
        xp[u, my_rows, :] = jnp.concatenate(parts, axis=0).astype(BF16)

    class Gather:
        IDX = {
            (0, -1, "AB"): 0,
            (0, 1, "AB"): 1,
            (0, 2, "AB"): 2,
            (1, 0, "AB"): 3,
            (1, -1, "A"): 4,
            (1, -1, "B"): 5,
            (1, 1, "A"): 6,
            (1, 1, "B"): 7,
            (1, 2, "A"): 8,
            (1, 2, "B"): 9,
        }

        def __init__(self, buf, i, par, u, cols):
            self.buf, self.i, self.u = buf, i, u
            self.par = par
            self.start, self.width, self.cut = cols

        def area(self, rows):
            return self.buf.at[self.u, rows, pl.ds(self.start, self.width)]

        def piece(self, s, e, part="AB"):
            rr = r_x if s == 0 else 1 - r_x
            slot = (rr * 2 + k) * 4 + (y + e + 4) % 4
            cols = pl.ds(self.start, self.width)
            if part == "A":
                cols = pl.ds(self.start, self.cut)
            elif part == "B":
                cols = pl.ds(self.start + self.cut, self.width - self.cut)
            return self.buf.at[self.u, rows_at(slot * ROWS, ROWS), cols]

        def rsem(self, *key):
            return sem_ag.at[self.i, self.IDX[key]]

        def send(self, s, e, part, device, key):
            ref = self.piece(s, e, part)
            rdma(ref, ref, sem_agd.at[self.i, 0], self.rsem(*key), device).start()

        def side(self, s, kk):
            rr = r_x if s == 0 else 1 - r_x
            return self.area(rows_at((rr * 2 + kk) * SIDE, SIDE))

        def to_sib(self, s):
            ref = self.side(s, k)
            rdma(
                ref, ref, sem_agd.at[self.i, 1], sem_agd.at[self.i, 2 + s], sib
            ).start()

        def wait(self, s, e, part):
            wait_bytes(self.piece(s, e, part), self.rsem(s, e, part))

        def o(self):
            self.send(0, 0, "AB", ring[1], (0, -1, "AB"))
            self.send(0, 0, "AB", ring[-1], (0, 1, "AB"))
            self.send(0, 0, "AB", pair, (1, 0, "AB"))

        def p(self):
            self.wait(1, 0, "AB")
            for s in (self.par, -self.par):
                self.send(1, 0, "B", ring[s], (1, -s, "B"))

        def first(self, e):
            self.wait(0, e, "AB")
            if e == -self.par:
                self.send(0, e, "AB", ring[self.par], (0, 2, "AB"))
            self.send(0, e, "A", pair, (1, e, "A"))

        def m(self):
            self.first(-1)

        def q(self):
            self.first(1)

        def b(self):
            self.wait(1, -self.par, "B")
            self.send(1, -self.par, "B", ring[self.par], (1, 2, "B"))

        def r(self):
            self.wait(0, 2, "AB")
            self.send(0, 2, "A", pair, (1, 2, "A"))
            self.to_sib(0)

        def e(self):
            self.wait(1, self.par, "B")
            for e in (-1, 1):
                self.wait(1, e, "A")
            self.wait(1, 2, "B")
            self.wait(1, 2, "A")
            self.to_sib(1)

        def here(self, s):
            wait_bytes(self.side(s, 1 - k), sem_agd.at[self.i, 2 + s])

        def sent(self):
            wait_bytes(self.area(pl.ds(0, 7 * ROWS)), sem_agd.at[self.i, 0])
            wait_bytes(self.area(pl.ds(0, 2 * SIDE)), sem_agd.at[self.i, 1])

    ax = [Gather(xp, u, 1 - 2 * (u % 2), u, X_PASS) for u in range(4)]
    steps = [z, (z + 3) % 4, (z + 1) % 4, (z + 2) % 4]
    ay = [
        [
            Gather(yp, 4 + 4 * n + t, 1 - 2 * (t % 2), steps[t], cols)
            for t in range(4)
        ]
        for n, cols in enumerate(Y_PASS)
    ]

    def side_start(c):
        return (r_x if c == 0 else 1 - r_x) * HB

    UNITS = ((0, 0, 512, 1), (0, 512, 384, -1), (1, 0, 512, -1), (1, 512, 384, 1))

    def unit_cols(c):
        side, start, n, _ = UNITS[c]
        return cols_at(side_start(side) + start, n)

    def partial_gram(u, c):
        side, start, n, s = UNITS[c]
        if start == 0:
            ax[u].here(side)
        tile = jnp.concatenate([xp[v, my_rows, :] for v in range(4)], axis=0)
        part = lax.dot_general(
            tile,
            xp[u, rows_at(side_start(side) + start, n), :],
            (((1,), (1,)), ((), ())),
            preferred_element_type=F32,
        ).astype(BF16)
        h = unit_cols(c)
        for v in range(4):
            pbuf[u, v, :, h] = part[v * ROWS : (v + 1) * ROWS]
        rs_send(pbuf.at[u, (z + 2) % 4, :, h], rbuf.at[u, 0, :, h], u, c, 0, zring[s])
        rs_send(
            pbuf.at[u, (z + 4 - s) % 4, :, h], rbuf.at[u, 1, :, h], u, c, 1, zring[-s]
        )

    def rs_send(src, dst, u, c, i, device):
        rdma(src, dst, sem_send.at[1, u], sem_rs.at[u * 4 + c, i], device).start()

    def rs_mid(u, c):
        s = UNITS[c][3]
        h = unit_cols(c)
        v = (z + 4 + s) % 4
        wait_bytes(rbuf.at[u, 0, :, h], sem_rs.at[u * 4 + c, 0])
        pbuf[u, v, :, h] = (
            pbuf[u, v, :, h].astype(F32) + rbuf[u, 0, :, h].astype(F32)
        ).astype(BF16)
        rs_send(pbuf.at[u, v, :, h], rbuf.at[u, 2, :, h], u, c, 2, zring[s])

    def rs_sum(u, c):
        h = unit_cols(c)
        wait_bytes(rbuf.at[u, 1, :, h], sem_rs.at[u * 4 + c, 1])
        wait_bytes(rbuf.at[u, 2, :, h], sem_rs.at[u * 4 + c, 2])
        pbuf[u, z, :, h] = (
            pbuf[u, z, :, h].astype(F32)
            + rbuf[u, 1, :, h].astype(F32)
            + rbuf[u, 2, :, h].astype(F32)
        ).astype(BF16)
        rs_send(pbuf.at[u, z, :, h], rx.at[u, :, h], u, c, 3, cpair)

    def rs_end(u, c):
        h = unit_cols(c)
        wait_bytes(rx.at[u, :, h], sem_rs.at[u * 4 + c, 3])
        total = pbuf[u, z, :, h].astype(F32) + rx[u, :, h].astype(F32)
        gb[z, u, :, h] = (total * inv_square).astype(BF16)

    def g_u(j):
        return c_x if j == 0 else j

    def gref(e, u, half=None):
        ref = gb.at[(z + e + 4) % 4, u]
        return ref if half is None else ref.at[:, pl.ds(half * HB, HB)]

    def g_send(ref, device, i):
        rdma(ref, ref, sem_send.at[2, 0], sem_g.at[i], device).start()

    def g_own(j):
        g_send(gref(0, g_u(j)), zring[1], 4 * j)
        g_send(gref(0, g_u(j)), zring[-1], 4 * j + 1)

    def g_pass(j, e):
        u = g_u(j)
        wait_bytes(gref(e, u), sem_g.at[4 * j + (0 if e == -1 else 1)])
        half = 0 if e == -1 else 1
        g_send(gref(e, u, half), zring[-e], 4 * j + 2 + half)
        if j == 0:
            g_send(gref(e, u), cpair, 16 + half)

    def g_far(j):
        for half in range(2):
            wait_bytes(gref(2, g_u(j), half), sem_g.at[4 * j + 2 + half])

    def g_far_pair():
        g_far(0)
        g_send(gref(2, g_u(0)), cpair, 18)

    def g_pair(e):
        wait_bytes(gref(e, 1 - c_x), sem_g.at[16 + (-1, 1, 2).index(e)])

    def first_prod(t):
        if t > 0:
            g_pair((0, -1, 1, 2)[t])
        if t == 3:
            g_far(2)
            g_far(3)
        v = steps[t]
        acc = zacc.at[pl.ds(0, ROWS)]
        acc[...] = jnp.dot(gb[v, 0], xp[0], preferred_element_type=F32)
        for u in range(1, 3):
            acc[...] += jnp.dot(gb[v, u], xp[u], preferred_element_type=F32)
        yp[v, my_rows, :] = (
            acc[...] + jnp.dot(gb[v, 3], xp[3], preferred_element_type=F32)
        ).astype(BF16)

    def second_prod(n, t):
        ay[n][t].here(0)
        ay[n][t].here(1)
        v = steps[t]
        cols = pl.ds(Y_PASS[n][0], Y_PASS[n][1])
        g = jnp.concatenate([gb[i, v] for i in range(4)], axis=0)
        term = jnp.dot(g, yp[v, :, cols], preferred_element_type=F32)
        if t == 0:
            zacc[:, cols] = term
        else:
            zacc[:, cols] += term

    def combine(n):
        cols = pl.ds(Y_PASS[n][0], Y_PASS[n][1])
        gap = jnp.zeros((PAD - HALF, Y_PASS[n][1]), F32)
        for v in range(4):
            it = (
                coef_a * xp[v, my_rows, cols].astype(F32)
                + coef_b * yp[v, my_rows, cols].astype(F32)
                + coef_c * zacc[pl.ds(v * ROWS, ROWS), cols]
            )
            for kk in range(2):
                fin[pl.ds((v * 2 + kk) * PAD, PAD), cols] = jnp.concatenate(
                    [it[kk * HALF : (kk + 1) * HALF], gap], axis=0
                ).astype(BF16)
        for device, zz, kk, self_too in way_back:
            move(
                fin.at[rows_at((zz * 2 + kk) * PAD, PAD), cols],
                out.at[rows_at((c_x * 4 + z) * PAD, PAD), cols],
                sem_send.at[3 + n, 1 if self_too else 0],
                sem_back.at[n, c_x * 4 + z],
                device,
                self_too,
            )

    def collect(n):
        start, width, _ = Y_PASS[n]
        for g in range(8):
            ref = fin.at[pl.ds(g * PAD, PAD), pl.ds(start, width)]
            wait_bytes(ref, sem_back.at[n, g])

    for name in ORDER:
        kind, args = name[0], [int(i) for i in name[1:] if i.isdigit()]
        if kind == "x":
            getattr(ax[args[0]], name[-1])()
        elif kind == "y":
            getattr(ay[args[0]][args[1]], name[-1])()
        elif kind in "ij":
            g_pass(args[0], -1 if kind == "i" else 1)
        else:
            {
                "a": assemble,
                "g": partial_gram,
                "s": rs_mid,
                "t": rs_sum,
                "w": rs_end,
                "h": g_own,
                "k": lambda _: g_far_pair(),
                "f": first_prod,
                "z": second_prod,
                "o": combine,
                "v": collect,
            }[kind](*args)

    for g in (*ax, *(g for n in ay for g in n)):
        g.sent()
    for u in range(4):
        wait_bytes(pbuf.at[u], sem_send.at[1, u])
    wait_bytes(gb.at[pl.ds(0, 3)], sem_send.at[2, 0])
    wait_bytes(ain.at[pl.ds(0, 7 * PAD)], sem_send.at[0, 0])
    for n, (start, width, _) in enumerate(Y_PASS):
        wait_bytes(
            fin.at[pl.ds(0, 7 * PAD), pl.ds(start, width)], sem_send.at[3 + n, 0]
        )

    @pl.when(jnp.logical_not(same))
    def _():
        wait_bytes(ain.at[pl.ds(0, PAD)], sem_send.at[0, 1])
        for n, (start, width, _) in enumerate(Y_PASS):
            wait_bytes(
                fin.at[pl.ds(0, PAD), pl.ds(start, width)], sem_send.at[3 + n, 1]
            )


def solution(mesh):
    def step(ortho_in):
        rows, full_cols = ortho_in.shape
        full_rows = rows * mesh.size
        inv_square = 1.0 / (math.sqrt(full_rows) + math.sqrt(full_cols)) ** 2
        vmem = pltpu.VMEM
        dma = pltpu.SemaphoreType.DMA
        n = len(Y_PASS)
        parts = pl.pallas_call(
            functools.partial(kernel, inv_square),
            name="newton_schulz",
            out_shape=jax.ShapeDtypeStruct((8 * PAD, PW), BF16),
            in_specs=[pl.BlockSpec(memory_space=pl.ANY)],
            out_specs=pl.BlockSpec(memory_space=pl.ANY),
            scratch_shapes=[
                vmem((HALF, 8 * PW), BF16),
                vmem((PAD, 8 * PW), BF16),
                vmem((8 * PAD, PW), BF16),
                vmem((4, BLK, PW), BF16),
                vmem((4, BLK, PW), BF16),
                vmem((4, 4, ROWS, BLK), BF16),
                vmem((4, 3, ROWS, BLK), BF16),
                vmem((4, ROWS, BLK), BF16),
                vmem((4, 4, ROWS, BLK), BF16),
                vmem((4 * ROWS, PW), F32),
                vmem((8 * PAD, PW), BF16),
                dma((1,)),
                dma((8,)),
                dma((4 + 4 * n, 10)),
                dma((4 + 4 * n, 4)),
                dma((16, 4)),
                dma((19,)),
                dma((n, 8)),
                dma((3 + n, 4)),
            ],
            compiler_params=pltpu.CompilerParams(
                collective_id=0,
                has_side_effects=True,
                vmem_limit_bytes=64 * 2**20 - 2**18,
            ),
            cost_estimate=pl.CostEstimate(
                flops=3 * 2 * 448 * 7168 * 1152,
                bytes_accessed=4 * 56 * 9216,
                transcendentals=0,
            ),
        )(ortho_in)
        parts = parts.reshape(8, PAD, PW)[:, :HALF]
        return parts.transpose(1, 0, 2).reshape(rows, full_cols)

    spec = P(("row", "col"), None)
    return jax.shard_map(
        step, mesh=mesh, in_specs=(spec,), out_specs=spec, check_vma=False
    )
```

```python
import functools
import math

import jax
import jax.numpy as jnp
from jax import lax
from jax.experimental import pallas as pl
from jax.experimental.pallas import tpu as pltpu
from jax.sharding import PartitionSpec as P

coef_a = 3.4445
coef_b = -4.775
coef_c = 2.0315

MESH = pl.DeviceIdType.MESH
F32 = jnp.float32
BF16 = jnp.bfloat16

STEPS = 7
T16 = 16
ROWS = STEPS * T16
HALF = 56
PAD = 64
PW = 1152
SEG = 256
BLK = 4 * SEG
UNIT = BLK // 2
X_PASS = (0, PW, 512)
Y_PASS = ((0, 512, 256), (512, 384, 128), (896, 256, 128))
RELAYED = (0, 2)

ORDER = (
    "a0", "a1", "x0o", "x1o", "a2", "a3", "x0m", "x0q", "x0p", "a4", "a5", "x1m", "x1q", "x1p",
    "a6", "x0r", "x2o", "x0b", "x1r", "g00", "x1b", "x3o", "g10", "x2m", "x2q", "x2p", "s00", "x0e",
    "x1e", "s10", "g01", "x3q", "g11", "t00", "x3p", "x3m", "x2r", "x4o", "t10", "s01", "x2b",
    "x3r", "g20", "w00", "x5o", "s11", "x3b", "g30", "w10", "t01", "x4m", "x4p", "x4q", "s20",
    "x2e", "s30", "x5q", "w01", "g21", "t11", "x3e", "t20", "x5p", "x5m", "x6o", "x4r", "g31",
    "t30", "s21", "x4b", "w11", "x5r", "g40", "x5b", "w20", "g50", "s31", "x6p", "x6m", "w30",
    "x6q", "t21", "s40", "x4e", "x5e", "x6b", "s50", "g41", "g51", "w21", "t40", "x6r", "t31",
    "t50", "g60", "x6e", "s41", "w40", "g61", "w31", "s51", "s60", "w50", "t41", "s61", "h2", "t60",
    "w41", "h4", "t51", "t61", "w60", "h0", "i2", "w51", "h5", "j2", "w61", "h6", "f0", "y00o",
    "i4", "j4", "i0", "y00m", "y00q", "y00p", "y10o", "j0", "y00r", "y10q", "y00b", "y10p", "i5",
    "j5", "y10m", "y20o", "y00e", "k2", "y10b", "y20q", "y20p", "i6", "f1", "y01o", "y11o", "j6",
    "f2", "y02o", "y10r", "y21o", "y01q", "k0", "y01p", "y01m", "y20m", "y20b", "y11m", "y11q",
    "y11p", "y02m", "y02p", "y02q", "y10e", "y21m", "y21q", "y21p", "f3", "y03o", "z00", "y01r",
    "y01b", "y11b", "y02r", "y11r", "z10", "y02b", "y12o", "y20r", "y21r", "y21b", "y03m", "y03p",
    "y03q", "y13o", "y01e", "y02e", "y12m", "y11e", "z01", "y12p", "y12q", "z02", "y03b", "y12r",
    "y20e", "y13m", "z11", "y12b", "y03r", "y22o", "y13p", "z20", "y21e", "y13q", "y23o", "y12e",
    "z21", "y03e", "y22m", "z12", "y22p", "y22q", "y13b", "z03", "o0", "y13r", "y22r", "y23p",
    "y23q", "y22b", "y23m", "y13e", "y23b", "y22e", "y23r", "z13", "o1", "z22", "y23e", "v0", "z23",
    "o2", "v1", "v2",
)


def kernel(
    inv_square,
    xin,
    out,
    xv,
    xl,
    ain,
    xp,
    yp,
    pbuf,
    rbuf,
    rx,
    gb,
    zacc,
    fin,
    sem_in,
    sem_a2a,
    sem_ag,
    sem_agd,
    sem_rs,
    sem_g,
    sem_back,
    sem_send,
):
    row, col = lax.axis_index("row"), lax.axis_index("col")
    k = row % 2
    y = (row // 2) % 4
    x = (col % 2) * 2 + row // 8
    z = col // 2
    r_x = ((x + 1) // 2) % 2
    c_x = x // 2

    def dev(xx, yy, zz, kk):
        return (((xx % 2) * 4 + yy) * 2 + kk, zz * 2 + xx // 2)

    x_row = x + 1 - 2 * (x % 2)
    x_col = 3 - x
    ring = {1: dev(x, (y + 1) % 4, z, k), -1: dev(x, (y + 3) % 4, z, k)}
    pair = dev(x_row, y, z, k)
    zring = {1: dev(x, y, (z + 1) % 4, k), -1: dev(x, y, (z + 3) % 4, k)}
    cpair = dev(x_col, y, z, k)
    sib = dev(x, y, z, 1 - k)
    same = k == c_x
    other = k + c_x - 2 * k * c_x
    x_far = x + (x_col - x) * other

    def rdma(src, dst, ssem, rsem, device):
        return pltpu.make_async_remote_copy(
            src_ref=src,
            dst_ref=dst,
            send_sem=ssem,
            recv_sem=rsem,
            device_id=device,
            device_id_type=MESH,
        )

    def wait_bytes(ref, sem):
        pltpu.make_async_copy(ref, ref, sem).wait()

    def rows_at(start, n):
        return pl.ds(pl.multiple_of(start, 16), n)

    def cols_at(start, n):
        return pl.ds(pl.multiple_of(start, 128), n)

    def move(src, dst, ssem, rsem, device, self_too):
        if not self_too:
            rdma(src, dst, ssem, rsem, device).start()
            return

        @pl.when(same)
        def _():
            pltpu.make_async_copy(src, dst, rsem).start()

        @pl.when(jnp.logical_not(same))
        def _():
            rdma(src, dst, ssem, rsem, device).start()

    load = pltpu.make_async_copy(xin, xv, sem_in.at[0])
    load.start()

    barrier = pltpu.get_barrier_semaphore()

    def greet(device):
        pl.semaphore_signal(barrier, inc=1, device_id=device, device_id_type=MESH)

    way_in = []
    for d in (0, 1, 3, 2):
        for i in range(2):
            xx, cc = (x, c_x) if i == 0 else (x_col, 1 - c_x)
            zz = (z + d) % 4
            way_in.append((dev(xx, y, zz, c_x), cc, zz, d == 0 and i == 0))
    way_back = []
    for d in (2, 1, 3, 0):
        for i in range(2):
            kk = k if i == 0 else 1 - k
            zz = (z + d) % 4
            way_back.append((dev(x_far, y, zz, kk), zz, kk, d == 0 and i == 0))
    for d in (ring[1], ring[-1], pair, sib):
        greet(d)
    for d, _, _, self_too in way_back:
        if not self_too:
            greet(d)
    back_self = way_back[-2][0]

    @pl.when(jnp.logical_not(same))
    def _():
        greet(back_self)

    pl.semaphore_wait(barrier, 11 + other)

    my_slot = (r_x * 2 + k) * 4 + y

    def slot_rows(slot):
        return rows_at(slot * T16, T16)

    their_slot = slot_rows((r_x * 2 + c_x) * 4 + y)

    def distribute(i):
        for device, cc, zz, self_too in way_in:
            cols = cols_at((cc * 4 + zz) * PW, PW)
            if i < 3:
                src = xin.at[pl.ds(i * T16, T16), cols]
                dst = xp.at[2 * i + k, z, their_slot]
                sem = sem_a2a.at[2 * i + k]
            else:
                src = xl.at[:, cols]
                dst = ain.at[z * 2 + k]
                sem = sem_a2a.at[6]
            move(src, dst, sem_send.at[0, 1 if self_too else 0], sem, device, self_too)

    for i in range(3):
        distribute(i)
    load.wait()
    xl[...] = jnp.concatenate(
        [xv[...].astype(F32)[48:], jnp.zeros((8, 8 * PW), F32)], axis=0
    ).astype(BF16)
    distribute(3)

    def assemble(u):
        if u < 6:
            wait_bytes(xp.at[u, :, slot_rows(my_slot)], sem_a2a.at[u])
            return
        wait_bytes(ain, sem_a2a.at[6])
        for v in range(4):
            xp[6, v, slot_rows(my_slot), :] = jnp.concatenate(
                [ain[v * 2 + kk].astype(F32)[:8] for kk in range(2)], axis=0
            ).astype(BF16)

    class Gather:
        IDX = {
            (0, -1, "AB"): 0,
            (0, 1, "AB"): 1,
            (0, 2, "AB"): 2,
            (1, 0, "AB"): 3,
            (1, -1, "A"): 4,
            (1, -1, "B"): 5,
            (1, 1, "A"): 6,
            (1, 1, "B"): 7,
            (1, 2, "A"): 8,
            (1, 2, "B"): 9,
        }

        def __init__(self, i, par, cols, area, whole):
            self.i, self.par, self.area, self.whole = i, par, area, whole
            self.start, self.width, self.cut = cols

        def piece(self, s, e, part="AB"):
            rr = r_x if s == 0 else 1 - r_x
            slot = (rr * 2 + k) * 4 + (y + e + 4) % 4
            cols = pl.ds(self.start, self.width)
            if part == "A":
                cols = pl.ds(self.start, self.cut)
            elif part == "B":
                cols = pl.ds(self.start + self.cut, self.width - self.cut)
            return self.area(slot_rows(slot), cols)

        def rsem(self, *key):
            return sem_ag.at[self.i, self.IDX[key]]

        def send(self, s, e, part, device, key):
            ref = self.piece(s, e, part)
            rdma(ref, ref, sem_agd.at[self.i, 0], self.rsem(*key), device).start()

        def side(self, s, kk):
            rr = r_x if s == 0 else 1 - r_x
            return self.area(
                rows_at((rr * 2 + kk) * 4 * T16, 4 * T16),
                pl.ds(self.start, self.width),
            )

        def to_sib(self, s):
            ref = self.side(s, k)
            rdma(
                ref, ref, sem_agd.at[self.i, 1], sem_agd.at[self.i, 2 + s], sib
            ).start()

        def wait(self, s, e, part):
            wait_bytes(self.piece(s, e, part), self.rsem(s, e, part))

        def o(self):
            self.send(0, 0, "AB", ring[1], (0, -1, "AB"))
            self.send(0, 0, "AB", ring[-1], (0, 1, "AB"))
            self.send(0, 0, "AB", pair, (1, 0, "AB"))

        def p(self):
            self.wait(1, 0, "AB")
            for s in (self.par, -self.par):
                self.send(1, 0, "B", ring[s], (1, -s, "B"))

        def first(self, e):
            self.wait(0, e, "AB")
            if e == -self.par:
                self.send(0, e, "AB", ring[self.par], (0, 2, "AB"))
            self.send(0, e, "A", pair, (1, e, "A"))

        def m(self):
            self.first(-1)

        def q(self):
            self.first(1)

        def b(self):
            self.wait(1, -self.par, "B")
            self.send(1, -self.par, "B", ring[self.par], (1, 2, "B"))

        def r(self):
            self.wait(0, 2, "AB")
            self.send(0, 2, "A", pair, (1, 2, "A"))
            self.to_sib(0)

        def e(self):
            self.wait(1, self.par, "B")
            for e in (-1, 1):
                self.wait(1, e, "A")
            self.wait(1, 2, "B")
            self.wait(1, 2, "A")
            self.to_sib(1)

        def here(self, s):
            wait_bytes(self.side(s, 1 - k), sem_agd.at[self.i, 2 + s])

        def sent(self):
            cols = pl.ds(self.start, self.width)
            wait_bytes(self.whole(cols), sem_agd.at[self.i, 0])
            wait_bytes(self.area(pl.ds(0, 8 * T16), cols), sem_agd.at[self.i, 1])

    def x_gather(u):
        return Gather(
            u,
            1 - 2 * (u % 2),
            X_PASS,
            lambda rows, cols: xp.at[u, :, rows, cols],
            lambda cols: xp.at[u, :, pl.ds(0, 7 * T16), cols],
        )

    def y_gather(n, t):
        return Gather(
            STEPS + 4 * n + t,
            1 - 2 * (t % 2),
            Y_PASS[n],
            lambda rows, cols: yp.at[:, steps[t], rows, cols],
            lambda cols: yp.at[:, 0, pl.ds(0, 7 * T16), cols],
        )

    steps = [z, (z + 3) % 4, (z + 1) % 4, (z + 2) % 4]
    ax = [x_gather(u) for u in range(STEPS)]
    ay = [[y_gather(n, t) for t in range(4)] for n in range(len(Y_PASS))]

    def side_rows(c):
        rr = r_x if c == 0 else 1 - r_x
        return rows_at(rr * 128, 128)

    def partial_gram(u, c):
        ax[u].here(c)
        tile = jnp.concatenate(
            [
                xp[i, v, slot_rows(my_slot), :]
                for v in range(4)
                for i in range(STEPS)
            ],
            axis=0,
        )
        part = lax.dot_general(
            tile,
            xp[u, :, side_rows(c), :].reshape(UNIT, PW),
            (((1,), (1,)), ((), ())),
            preferred_element_type=F32,
        ).astype(BF16)
        for v in range(4):
            pbuf[u, c, v] = part[v * ROWS : (v + 1) * ROWS]
        s = 1 if c == 0 else -1
        rs_send(pbuf.at[u, c, (z + 2) % 4], rbuf.at[u, c, 0], u, c, 0, zring[s])
        rs_send(pbuf.at[u, c, (z + 4 - s) % 4], rbuf.at[u, c, 1], u, c, 1, zring[-s])

    def rs_send(src, dst, u, c, i, device):
        rdma(src, dst, sem_send.at[1, u], sem_rs.at[u * 2 + c, i], device).start()

    def rs_mid(u, c):
        s = 1 if c == 0 else -1
        v = (z + 4 + s) % 4
        wait_bytes(rbuf.at[u, c, 0], sem_rs.at[u * 2 + c, 0])
        pbuf[u, c, v] = (
            pbuf[u, c, v].astype(F32) + rbuf[u, c, 0].astype(F32)
        ).astype(BF16)
        rs_send(pbuf.at[u, c, v], rbuf.at[u, c, 2], u, c, 2, zring[s])

    def rs_sum(u, c):
        wait_bytes(rbuf.at[u, c, 1], sem_rs.at[u * 2 + c, 1])
        wait_bytes(rbuf.at[u, c, 2], sem_rs.at[u * 2 + c, 2])
        pbuf[u, c, z] = (
            pbuf[u, c, z].astype(F32)
            + rbuf[u, c, 1].astype(F32)
            + rbuf[u, c, 2].astype(F32)
        ).astype(BF16)
        rs_send(pbuf.at[u, c, z], rx.at[u, c], u, c, 3, cpair)

    def rs_end(u, c):
        wait_bytes(rx.at[u, c], sem_rs.at[u * 2 + c, 3])
        total = pbuf[u, c, z].astype(F32) + rx[u, c].astype(F32)
        done = (total * inv_square).astype(BF16)
        rr = r_x if c == 0 else 1 - r_x
        for v in range(4):
            gb[z, u, :, cols_at(v * SEG + rr * 128, 128)] = done[
                :, v * 128 : (v + 1) * 128
            ]

    CLASSES = list(RELAYED) + [
        b for b in range(STEPS) if b not in RELAYED and b - 1 not in RELAYED
    ]

    def g_u(b):
        return b + c_x if b in RELAYED else b

    def gref(e, u, half=None):
        ref = gb.at[(z + e + 4) % 4, u]
        return ref if half is None else ref.at[:, pl.ds(half * UNIT, UNIT)]

    def g_send(ref, device, b, i):
        rdma(ref, ref, sem_send.at[2, 0], sem_g.at[b, i], device).start()

    def g_own(b):
        g_send(gref(0, g_u(b)), zring[1], b, 0)
        g_send(gref(0, g_u(b)), zring[-1], b, 1)

    def g_pass(b, e):
        u = g_u(b)
        half = 0 if e == -1 else 1
        wait_bytes(gref(e, u), sem_g.at[b, half])
        g_send(gref(e, u, half), zring[-e], b, 2 + half)
        if b in RELAYED:
            g_send(gref(e, u), cpair, b, 4 + half)

    def g_far(b):
        for half in range(2):
            wait_bytes(gref(2, g_u(b), half), sem_g.at[b, 2 + half])

    def g_far_pair(b):
        g_far(b)
        g_send(gref(2, g_u(b)), cpair, b, 6)

    def first_prod(t):
        e = (0, -1, 1, 2)[t]
        if t > 0:
            for b in RELAYED:
                wait_bytes(gref(e, b + 1 - c_x), sem_g.at[b, 3 + t])
        if t == 3:
            for b in CLASSES:
                if b not in RELAYED:
                    g_far(b)
        v = steps[t]
        acc = zacc.at[pl.ds(0, ROWS)]
        for u in range(STEPS):
            term = jnp.dot(
                gb[v, u], xp[u].reshape(BLK, PW), preferred_element_type=F32
            )
            if u == 0:
                acc[...] = term
            else:
                acc[...] += term
        for i in range(STEPS):
            yp[i, v, slot_rows(my_slot), :] = acc[pl.ds(i * T16, T16), :].astype(BF16)

    def second_prod(n, t):
        ay[n][t].here(0)
        ay[n][t].here(1)
        v = steps[t]
        cols = pl.ds(Y_PASS[n][0], Y_PASS[n][1])
        g = jnp.concatenate(
            [
                jnp.concatenate(
                    [gb[j, i, :, cols_at(v * SEG, SEG)] for i in range(STEPS)], axis=1
                )
                for j in range(4)
            ],
            axis=0,
        )
        term = jnp.dot(
            g,
            yp[:, v, :, cols].reshape(STEPS * SEG, Y_PASS[n][1]),
            preferred_element_type=F32,
        )
        if t == 0:
            zacc[:, cols] = term
        else:
            zacc[:, cols] += term

    def combine(n):
        cols = pl.ds(Y_PASS[n][0], Y_PASS[n][1])
        gap = jnp.zeros((PAD - HALF, Y_PASS[n][1]), F32)
        for v in range(4):
            it = [
                coef_a * xp[i, v, slot_rows(my_slot), cols].astype(F32)
                + coef_b * yp[i, v, slot_rows(my_slot), cols].astype(F32)
                + coef_c * zacc[pl.ds(v * ROWS + i * T16, T16), cols]
                for i in range(STEPS)
            ]
            for kk in range(2):
                mine = [it[kk], it[kk + 2], it[kk + 4], it[6][kk * 8 : kk * 8 + 8], gap]
                fin[pl.ds((v * 2 + kk) * PAD, PAD), cols] = jnp.concatenate(
                    mine, axis=0
                ).astype(BF16)
        for device, zz, kk, self_too in way_back:
            move(
                fin.at[rows_at((zz * 2 + kk) * PAD, PAD), cols],
                out.at[rows_at((c_x * 4 + z) * PAD, PAD), cols],
                sem_send.at[3 + n, 1 if self_too else 0],
                sem_back.at[n, c_x * 4 + z],
                device,
                self_too,
            )

    def collect(n):
        start, width, _ = Y_PASS[n]
        for g in range(8):
            ref = fin.at[pl.ds(g * PAD, PAD), pl.ds(start, width)]
            wait_bytes(ref, sem_back.at[n, g])

    for name in ORDER:
        kind, args = name[0], [int(i) for i in name[1:] if i.isdigit()]
        if kind == "x":
            getattr(ax[args[0]], name[-1])()
        elif kind == "y":
            getattr(ay[args[0]][args[1]], name[-1])()
        elif kind in "ij":
            g_pass(args[0], -1 if kind == "i" else 1)
        else:
            {
                "a": assemble,
                "g": partial_gram,
                "s": rs_mid,
                "t": rs_sum,
                "w": rs_end,
                "h": g_own,
                "k": g_far_pair,
                "f": first_prod,
                "z": second_prod,
                "o": combine,
                "v": collect,
            }[kind](*args)

    for g in (*ax, *(g for n in ay for g in n)):
        g.sent()
    for u in range(STEPS):
        wait_bytes(pbuf.at[u], sem_send.at[1, u])
    wait_bytes(gb.at[pl.ds(0, 3)], sem_send.at[2, 0])
    wait_bytes(yp.at[0, pl.ds(0, 2), pl.ds(0, 7 * 32)], sem_send.at[0, 0])
    for n, (start, width, _) in enumerate(Y_PASS):
        wait_bytes(
            fin.at[pl.ds(0, 7 * PAD), pl.ds(start, width)], sem_send.at[3 + n, 0]
        )

    @pl.when(jnp.logical_not(same))
    def _():
        wait_bytes(yp.at[0, 0, pl.ds(0, PAD)], sem_send.at[0, 1])
        for n, (start, width, _) in enumerate(Y_PASS):
            wait_bytes(
                fin.at[pl.ds(0, PAD), pl.ds(start, width)], sem_send.at[3 + n, 1]
            )


def solution(mesh):
    def step(ortho_in):
        rows, full_cols = ortho_in.shape
        full_rows = rows * mesh.size
        inv_square = 1.0 / (math.sqrt(full_rows) + math.sqrt(full_cols)) ** 2
        vmem = pltpu.VMEM
        dma = pltpu.SemaphoreType.DMA
        n = len(Y_PASS)
        parts = pl.pallas_call(
            functools.partial(kernel, inv_square),
            name="newton_schulz",
            out_shape=jax.ShapeDtypeStruct((8 * PAD, PW), BF16),
            in_specs=[pl.BlockSpec(memory_space=pl.ANY)],
            out_specs=pl.BlockSpec(memory_space=pl.ANY),
            scratch_shapes=[
                vmem((HALF, 8 * PW), BF16),
                vmem((T16, 8 * PW), BF16),
                vmem((8, T16, PW), BF16),
                vmem((STEPS, 4, SEG, PW), BF16),
                vmem((STEPS, 4, SEG, PW), BF16),
                vmem((STEPS, 2, 4, ROWS, UNIT), BF16),
                vmem((STEPS, 2, 3, ROWS, UNIT), BF16),
                vmem((STEPS, 2, ROWS, UNIT), BF16),
                vmem((4, STEPS, ROWS, BLK), BF16),
                vmem((4 * ROWS, PW), F32),
                vmem((8 * PAD, PW), BF16),
                dma((1,)),
                dma((STEPS,)),
                dma((STEPS + 4 * n, 10)),
                dma((STEPS + 4 * n, 4)),
                dma((2 * STEPS, 4)),
                dma((STEPS, 7)),
                dma((n, 8)),
                dma((3 + n, 8)),
            ],
            compiler_params=pltpu.CompilerParams(
                collective_id=0,
                has_side_effects=True,
                vmem_limit_bytes=64 * 2**20 - 2**18,
            ),
            cost_estimate=pl.CostEstimate(
                flops=3 * 2 * 448 * 7168 * 1152,
                bytes_accessed=4 * 56 * 9216,
                transcendentals=0,
            ),
        )(ortho_in)
        parts = parts.reshape(8, PAD, PW)[:, :HALF]
        return parts.transpose(1, 0, 2).reshape(rows, full_cols)

    spec = P(("row", "col"), None)
    return jax.shard_map(
        step, mesh=mesh, in_specs=(spec,), out_specs=spec, check_vma=False
    )
```

```python
import functools
import math

import jax
import jax.numpy as jnp
from jax import lax
from jax.experimental import pallas as pl
from jax.experimental.pallas import tpu as pltpu
from jax.sharding import PartitionSpec as P

coef_a = 3.4445
coef_b = -4.775
coef_c = 2.0315

MESH = pl.DeviceIdType.MESH
F32 = jnp.float32
BF16 = jnp.bfloat16

STEPS = 7
T16 = 16
ROWS = STEPS * T16
HALF = 56
PAD = 64
PW = 1152
SEG = 256
BLK = 4 * SEG
UNIT = BLK // 2
X_PASS = (0, PW, 512)
Y_PASS = ((0, 512, 256), (512, 384, 128), (896, 256, 128))
RELAYED = (2, 4)

ORDER = (
    "a0", "x0o", "a1", "x1o", "x0m", "a5", "x0p", "x1q", "x1p", "a6", "a4", "x1m", "x0q", "a3",
    "a2", "x0r", "x2o", "x0b", "x1r", "g00", "x1b", "g10", "x3o", "s00", "x0e", "x2m", "x2p", "s10",
    "x1e", "g01", "x3q", "x2q", "x3p", "g11", "x2r", "x3m", "x4o", "s01", "x3r", "g20", "t10",
    "x2b", "x3b", "s11", "x5o", "g30", "s20", "x2e", "x4m", "x4p", "x3e", "s30", "x4q", "g21",
    "x5q", "t00", "x5p", "g31", "x4r", "x5m", "x6o", "s21", "t11", "t20", "x5r", "g40", "x4b",
    "x5b", "g50", "t30", "w10", "x6m", "t01", "s31", "x4e", "s40", "x6q", "x5e", "x6p", "s50",
    "w20", "g41", "x6r", "t21", "w30", "g51", "x6b", "g60", "t31", "t50", "x6e", "s41", "w11",
    "g61", "s51", "s60", "t40", "w21", "t41", "w31", "s61", "h1", "h2", "t51", "t61", "t60", "w40",
    "w41", "w00", "w50", "w01", "w51", "h4", "l0", "h0", "w61", "w60", "h6", "i2", "i1", "f0",
    "y00o", "y10o", "y20o", "i4", "y00m", "y10m", "j2", "i0", "y10p", "j4", "y00q", "y20q", "y20m",
    "y20p", "y00p", "y00r", "l1", "i6", "f1", "y11o", "j1", "y01o", "y21o", "j0", "y10q", "y10b",
    "y00b", "k2", "y20r", "y10r", "j6", "y11p", "y20b", "y01q", "y11q", "l2", "y01m", "k4", "f2",
    "y02o", "y01p", "y20e", "y10e", "y11b", "y01r", "y11m", "y00e", "y11r", "y02m", "y02q", "y02p",
    "y12o", "l3", "y01b", "f3", "y03o", "y02r", "z10", "y21p", "y02b", "y12m", "y12p", "z00",
    "y03p", "y21m", "y12q", "y01e", "y11e", "y03q", "y03m", "y13o", "z20", "z01", "y02e", "y12b",
    "y03b", "y03r", "y12r", "y22o", "z02", "y13p", "y13q", "y13m", "y23o", "y03e", "z11", "y22m",
    "y22q", "y12e", "y13b", "y21q", "z03", "y13r", "y23p", "y23m", "o0", "y23q", "y22p", "y22r",
    "y13e", "z12", "y21r", "y21b", "y23b", "y22b", "z13", "y23r", "o1", "y21e", "y22e", "y23e",
    "z21", "z22", "z23", "o2", "v0", "v1", "v2",
)


def kernel(
    inv_square,
    xin,
    out,
    xv,
    xl,
    ain,
    xp,
    yp,
    pbuf,
    rbuf,
    rx,
    gb,
    zacc,
    fin,
    sem_in,
    sem_a2a,
    sem_ag,
    sem_agd,
    sem_rs,
    sem_g,
    sem_back,
    sem_send,
):
    row, col = lax.axis_index("row"), lax.axis_index("col")
    k = row % 2
    y = (row // 2) % 4
    x = (col % 2) * 2 + row // 8
    z = col // 2
    r_x = ((x + 1) // 2) % 2
    c_x = x // 2

    def dev(xx, yy, zz, kk):
        return (((xx % 2) * 4 + yy) * 2 + kk, zz * 2 + xx // 2)

    x_row = x + 1 - 2 * (x % 2)
    x_col = 3 - x
    ring = {1: dev(x, (y + 1) % 4, z, k), -1: dev(x, (y + 3) % 4, z, k)}
    pair = dev(x_row, y, z, k)
    zring = {1: dev(x, y, (z + 1) % 4, k), -1: dev(x, y, (z + 3) % 4, k)}
    cpair = dev(x_col, y, z, k)
    sib = dev(x, y, z, 1 - k)
    same = k == c_x
    other = k + c_x - 2 * k * c_x
    x_far = x + (x_col - x) * other

    def rdma(src, dst, ssem, rsem, device):
        return pltpu.make_async_remote_copy(
            src_ref=src,
            dst_ref=dst,
            send_sem=ssem,
            recv_sem=rsem,
            device_id=device,
            device_id_type=MESH,
        )

    def wait_bytes(ref, sem):
        pltpu.make_async_copy(ref, ref, sem).wait()

    def rows_at(start, n):
        return pl.ds(pl.multiple_of(start, 16), n)

    def cols_at(start, n):
        return pl.ds(pl.multiple_of(start, 128), n)

    def move(src, dst, ssem, rsem, device, self_too):
        if not self_too:
            rdma(src, dst, ssem, rsem, device).start()
            return

        @pl.when(same)
        def _():
            pltpu.make_async_copy(src, dst, rsem).start()

        @pl.when(jnp.logical_not(same))
        def _():
            rdma(src, dst, ssem, rsem, device).start()

    load = pltpu.make_async_copy(xin, xv, sem_in.at[0])
    load.start()

    barrier = pltpu.get_barrier_semaphore()

    def greet(device):
        pl.semaphore_signal(barrier, inc=1, device_id=device, device_id_type=MESH)

    way_in = []
    for d in (0, 1, 3, 2):
        for i in range(2):
            xx, cc = (x, c_x) if i == 0 else (x_col, 1 - c_x)
            zz = (z + d) % 4
            way_in.append((dev(xx, y, zz, c_x), cc, zz, d == 0 and i == 0))
    way_back = []
    for d in (2, 1, 3, 0):
        for i in range(2):
            kk = k if i == 0 else 1 - k
            zz = (z + d) % 4
            way_back.append((dev(x_far, y, zz, kk), zz, kk, d == 0 and i == 0))
    for d in (ring[1], ring[-1], pair, sib):
        greet(d)
    for d, _, _, self_too in way_back:
        if not self_too:
            greet(d)
    back_self = way_back[-2][0]

    @pl.when(jnp.logical_not(same))
    def _():
        greet(back_self)

    pl.semaphore_wait(barrier, 11 + other)

    my_slot = (r_x * 2 + k) * 4 + y

    def slot_rows(slot):
        return rows_at(slot * T16, T16)

    their_slot = slot_rows((r_x * 2 + c_x) * 4 + y)

    def distribute(i):
        for device, cc, zz, self_too in way_in:
            cols = cols_at((cc * 4 + zz) * PW, PW)
            if i < 3:
                src = xin.at[pl.ds(i * T16, T16), cols]
                dst = xp.at[2 * i + k, z, their_slot]
                sem = sem_a2a.at[2 * i + k]
            else:
                src = xl.at[:, cols]
                dst = ain.at[z * 2 + k]
                sem = sem_a2a.at[6]
            move(src, dst, sem_send.at[0, 1 if self_too else 0], sem, device, self_too)

    for i in range(3):
        distribute(i)
    load.wait()
    xl[...] = jnp.concatenate(
        [xv[...].astype(F32)[48:], jnp.zeros((8, 8 * PW), F32)], axis=0
    ).astype(BF16)
    distribute(3)

    def assemble(u):
        if u < 6:
            wait_bytes(xp.at[u, :, slot_rows(my_slot)], sem_a2a.at[u])
            return
        wait_bytes(ain, sem_a2a.at[6])
        for v in range(4):
            xp[6, v, slot_rows(my_slot), :] = jnp.concatenate(
                [ain[v * 2 + kk].astype(F32)[:8] for kk in range(2)], axis=0
            ).astype(BF16)

    class Gather:
        IDX = {
            (0, -1, "AB"): 0,
            (0, 1, "AB"): 1,
            (0, 2, "AB"): 2,
            (1, 0, "AB"): 3,
            (1, -1, "A"): 4,
            (1, -1, "B"): 5,
            (1, 1, "A"): 6,
            (1, 1, "B"): 7,
            (1, 2, "A"): 8,
            (1, 2, "B"): 9,
        }

        def __init__(self, i, par, cols, area, whole):
            self.i, self.par, self.area, self.whole = i, par, area, whole
            self.start, self.width, self.cut = cols

        def piece(self, s, e, part="AB"):
            rr = r_x if s == 0 else 1 - r_x
            slot = (rr * 2 + k) * 4 + (y + e + 4) % 4
            cols = pl.ds(self.start, self.width)
            if part == "A":
                cols = pl.ds(self.start, self.cut)
            elif part == "B":
                cols = pl.ds(self.start + self.cut, self.width - self.cut)
            return self.area(slot_rows(slot), cols)

        def rsem(self, *key):
            return sem_ag.at[self.i, self.IDX[key]]

        def send(self, s, e, part, device, key):
            ref = self.piece(s, e, part)
            rdma(ref, ref, sem_agd.at[self.i, 0], self.rsem(*key), device).start()

        def side(self, s, kk):
            rr = r_x if s == 0 else 1 - r_x
            return self.area(
                rows_at((rr * 2 + kk) * 4 * T16, 4 * T16),
                pl.ds(self.start, self.width),
            )

        def to_sib(self, s):
            ref = self.side(s, k)
            rdma(
                ref, ref, sem_agd.at[self.i, 1], sem_agd.at[self.i, 2 + s], sib
            ).start()

        def wait(self, s, e, part):
            wait_bytes(self.piece(s, e, part), self.rsem(s, e, part))

        def o(self):
            self.send(0, 0, "AB", ring[1], (0, -1, "AB"))
            self.send(0, 0, "AB", ring[-1], (0, 1, "AB"))
            self.send(0, 0, "AB", pair, (1, 0, "AB"))

        def p(self):
            self.wait(1, 0, "AB")
            for s in (self.par, -self.par):
                self.send(1, 0, "B", ring[s], (1, -s, "B"))

        def first(self, e):
            self.wait(0, e, "AB")
            if e == -self.par:
                self.send(0, e, "AB", ring[self.par], (0, 2, "AB"))
            self.send(0, e, "A", pair, (1, e, "A"))

        def m(self):
            self.first(-1)

        def q(self):
            self.first(1)

        def b(self):
            self.wait(1, -self.par, "B")
            self.send(1, -self.par, "B", ring[self.par], (1, 2, "B"))

        def r(self):
            self.wait(0, 2, "AB")
            self.send(0, 2, "A", pair, (1, 2, "A"))
            self.to_sib(0)

        def e(self):
            self.wait(1, self.par, "B")
            for e in (-1, 1):
                self.wait(1, e, "A")
            self.wait(1, 2, "B")
            self.wait(1, 2, "A")
            self.to_sib(1)

        def here(self, s):
            wait_bytes(self.side(s, 1 - k), sem_agd.at[self.i, 2 + s])

        def sent(self):
            cols = pl.ds(self.start, self.width)
            wait_bytes(self.whole(cols), sem_agd.at[self.i, 0])
            wait_bytes(self.area(pl.ds(0, 8 * T16), cols), sem_agd.at[self.i, 1])

    def x_gather(u):
        return Gather(
            u,
            1 - 2 * (u % 2),
            X_PASS,
            lambda rows, cols: xp.at[u, :, rows, cols],
            lambda cols: xp.at[u, :, pl.ds(0, 7 * T16), cols],
        )

    def y_gather(n, t):
        return Gather(
            STEPS + 4 * n + t,
            1 - 2 * (t % 2),
            Y_PASS[n],
            lambda rows, cols: yp.at[:, steps[t], rows, cols],
            lambda cols: yp.at[:, 0, pl.ds(0, 7 * T16), cols],
        )

    steps = [z, (z + 3) % 4, (z + 1) % 4, (z + 2) % 4]
    ax = [x_gather(u) for u in range(STEPS)]
    ay = [[y_gather(n, t) for t in range(4)] for n in range(len(Y_PASS))]

    def side_rows(c):
        rr = r_x if c == 0 else 1 - r_x
        return rows_at(rr * 128, 128)

    def partial_gram(u, c):
        ax[u].here(c)
        tile = jnp.concatenate(
            [
                xp[i, v, slot_rows(my_slot), :]
                for v in range(4)
                for i in range(STEPS)
            ],
            axis=0,
        )
        part = lax.dot_general(
            tile,
            xp[u, :, side_rows(c), :].reshape(UNIT, PW),
            (((1,), (1,)), ((), ())),
            preferred_element_type=F32,
        ).astype(BF16)
        for v in range(4):
            pbuf[u, c, v] = part[v * ROWS : (v + 1) * ROWS]
        s = 1 if c == 0 else -1
        rs_send(pbuf.at[u, c, (z + 2) % 4], rbuf.at[u, c, 0], u, c, 0, zring[s])
        rs_send(pbuf.at[u, c, (z + 4 - s) % 4], rbuf.at[u, c, 1], u, c, 1, zring[-s])

    def rs_send(src, dst, u, c, i, device):
        rdma(src, dst, sem_send.at[1, u], sem_rs.at[u * 2 + c, i], device).start()

    def rs_mid(u, c):
        s = 1 if c == 0 else -1
        v = (z + 4 + s) % 4
        wait_bytes(rbuf.at[u, c, 0], sem_rs.at[u * 2 + c, 0])
        pbuf[u, c, v] = (
            pbuf[u, c, v].astype(F32) + rbuf[u, c, 0].astype(F32)
        ).astype(BF16)
        rs_send(pbuf.at[u, c, v], rbuf.at[u, c, 2], u, c, 2, zring[s])

    def rs_sum(u, c):
        wait_bytes(rbuf.at[u, c, 1], sem_rs.at[u * 2 + c, 1])
        wait_bytes(rbuf.at[u, c, 2], sem_rs.at[u * 2 + c, 2])
        pbuf[u, c, z] = (
            pbuf[u, c, z].astype(F32)
            + rbuf[u, c, 1].astype(F32)
            + rbuf[u, c, 2].astype(F32)
        ).astype(BF16)
        rs_send(pbuf.at[u, c, z], rx.at[u, c], u, c, 3, cpair)

    def rs_end(u, c):
        wait_bytes(rx.at[u, c], sem_rs.at[u * 2 + c, 3])
        total = pbuf[u, c, z].astype(F32) + rx[u, c].astype(F32)
        done = (total * inv_square).astype(BF16)
        rr = r_x if c == 0 else 1 - r_x
        for v in range(4):
            gb[z, u, :, cols_at(v * SEG + rr * 128, 128)] = done[
                :, v * 128 : (v + 1) * 128
            ]

    CLASSES = list(RELAYED) + [
        b for b in range(STEPS) if b not in RELAYED and b - 1 not in RELAYED
    ]

    def g_u(b):
        return b + c_x if b in RELAYED else b

    def gref(e, u, half=None):
        ref = gb.at[(z + e + 4) % 4, u]
        return ref if half is None else ref.at[:, pl.ds(half * UNIT, UNIT)]

    def g_send(ref, device, b, i):
        rdma(ref, ref, sem_send.at[2, 0], sem_g.at[b, i], device).start()

    def g_own(b):
        g_send(gref(0, g_u(b)), zring[1], b, 0)
        g_send(gref(0, g_u(b)), zring[-1], b, 1)

    def g_pass(b, e):
        u = g_u(b)
        half = 0 if e == -1 else 1
        wait_bytes(gref(e, u), sem_g.at[b, half])
        g_send(gref(e, u, half), zring[-e], b, 2 + half)
        if b in RELAYED:
            g_send(gref(e, u), cpair, b, 4 + half)

    def g_far(b):
        for half in range(2):
            wait_bytes(gref(2, g_u(b), half), sem_g.at[b, 2 + half])

    def g_far_pair(b):
        g_far(b)
        g_send(gref(2, g_u(b)), cpair, b, 6)

    def first_prod(t, part):
        e = (0, -1, 1, 2)[t]
        if t > 0 and part == 0:
            for b in RELAYED:
                wait_bytes(gref(e, b + 1 - c_x), sem_g.at[b, 3 + t])
        if t == 3:
            for b in CLASSES:
                if b not in RELAYED and (b == STEPS - 1) == (part == 1):
                    g_far(b)
        v = steps[t]
        acc = zacc.at[pl.ds(t * ROWS, ROWS)]
        for u in range(STEPS - 1) if part == 0 else (STEPS - 1,):
            term = jnp.dot(
                gb[v, u], xp[u].reshape(BLK, PW), preferred_element_type=F32
            )
            if u == 0:
                acc[...] = term
            else:
                acc[...] += term
        if part == 1:
            for i in range(STEPS):
                yp[i, v, slot_rows(my_slot), :] = acc[pl.ds(i * T16, T16), :].astype(
                    BF16
                )

    def second_prod(n, t):
        ay[n][t].here(0)
        ay[n][t].here(1)
        v = steps[t]
        cols = pl.ds(Y_PASS[n][0], Y_PASS[n][1])
        g = jnp.concatenate(
            [
                jnp.concatenate(
                    [gb[j, i, :, cols_at(v * SEG, SEG)] for i in range(STEPS)], axis=1
                )
                for j in range(4)
            ],
            axis=0,
        )
        term = jnp.dot(
            g,
            yp[:, v, :, cols].reshape(STEPS * SEG, Y_PASS[n][1]),
            preferred_element_type=F32,
        )
        if t == 0:
            zacc[:, cols] = term
        else:
            zacc[:, cols] += term

    def combine(n):
        cols = pl.ds(Y_PASS[n][0], Y_PASS[n][1])
        gap = jnp.zeros((PAD - HALF, Y_PASS[n][1]), F32)
        for v in range(4):
            it = [
                coef_a * xp[i, v, slot_rows(my_slot), cols].astype(F32)
                + coef_b * yp[i, v, slot_rows(my_slot), cols].astype(F32)
                + coef_c * zacc[pl.ds(v * ROWS + i * T16, T16), cols]
                for i in range(STEPS)
            ]
            for kk in range(2):
                mine = [it[kk], it[kk + 2], it[kk + 4], it[6][kk * 8 : kk * 8 + 8], gap]
                fin[pl.ds((v * 2 + kk) * PAD, PAD), cols] = jnp.concatenate(
                    mine, axis=0
                ).astype(BF16)
        for device, zz, kk, self_too in way_back:
            move(
                fin.at[rows_at((zz * 2 + kk) * PAD, PAD), cols],
                out.at[:, cols_at((c_x * 4 + z) * PW + Y_PASS[n][0], Y_PASS[n][1])],
                sem_send.at[3 + n, 1 if self_too else 0],
                sem_back.at[n, c_x * 4 + z],
                device,
                self_too,
            )

    def collect(n):
        start, width, _ = Y_PASS[n]
        for g in range(8):
            ref = fin.at[pl.ds(g * PAD, PAD), pl.ds(start, width)]
            wait_bytes(ref, sem_back.at[n, g])

    for name in ORDER:
        kind, args = name[0], [int(i) for i in name[1:] if i.isdigit()]
        if kind == "x":
            getattr(ax[args[0]], name[-1])()
        elif kind == "y":
            getattr(ay[args[0]][args[1]], name[-1])()
        elif kind in "ij":
            g_pass(args[0], -1 if kind == "i" else 1)
        else:
            {
                "a": assemble,
                "g": partial_gram,
                "s": rs_mid,
                "t": rs_sum,
                "w": rs_end,
                "h": g_own,
                "k": g_far_pair,
                "l": lambda t: first_prod(t, 0),
                "f": lambda t: first_prod(t, 1),
                "z": second_prod,
                "o": combine,
                "v": collect,
            }[kind](*args)

    for g in (*ax, *(g for n in ay for g in n)):
        g.sent()
    for u in range(STEPS):
        wait_bytes(pbuf.at[u], sem_send.at[1, u])
    wait_bytes(gb.at[pl.ds(0, 3)], sem_send.at[2, 0])
    wait_bytes(yp.at[0, pl.ds(0, 2), pl.ds(0, 7 * 32)], sem_send.at[0, 0])
    for n, (start, width, _) in enumerate(Y_PASS):
        wait_bytes(
            fin.at[pl.ds(0, 7 * PAD), pl.ds(start, width)], sem_send.at[3 + n, 0]
        )

    @pl.when(jnp.logical_not(same))
    def _():
        wait_bytes(yp.at[0, 0, pl.ds(0, PAD)], sem_send.at[0, 1])
        for n, (start, width, _) in enumerate(Y_PASS):
            wait_bytes(
                fin.at[pl.ds(0, PAD), pl.ds(start, width)], sem_send.at[3 + n, 1]
            )


def solution(mesh):
    def step(ortho_in):
        rows, full_cols = ortho_in.shape
        full_rows = rows * mesh.size
        inv_square = 1.0 / (math.sqrt(full_rows) + math.sqrt(full_cols)) ** 2
        vmem = pltpu.VMEM
        dma = pltpu.SemaphoreType.DMA
        n = len(Y_PASS)
        padded = pl.pallas_call(
            functools.partial(kernel, inv_square),
            name="newton_schulz",
            out_shape=jax.ShapeDtypeStruct((PAD, full_cols), BF16),
            in_specs=[pl.BlockSpec(memory_space=pl.ANY)],
            out_specs=pl.BlockSpec(memory_space=pl.ANY),
            scratch_shapes=[
                vmem((HALF, 8 * PW), BF16),
                vmem((T16, 8 * PW), BF16),
                vmem((8, T16, PW), BF16),
                vmem((STEPS, 4, SEG, PW), BF16),
                vmem((STEPS, 4, SEG, PW), BF16),
                vmem((STEPS, 2, 4, ROWS, UNIT), BF16),
                vmem((STEPS, 2, 3, ROWS, UNIT), BF16),
                vmem((STEPS, 2, ROWS, UNIT), BF16),
                vmem((4, STEPS, ROWS, BLK), BF16),
                vmem((4 * ROWS, PW), F32),
                vmem((8 * PAD, PW), BF16),
                dma((1,)),
                dma((STEPS,)),
                dma((STEPS + 4 * n, 10)),
                dma((STEPS + 4 * n, 4)),
                dma((2 * STEPS, 4)),
                dma((STEPS, 7)),
                dma((n, 8)),
                dma((3 + n, 8)),
            ],
            compiler_params=pltpu.CompilerParams(
                collective_id=0,
                has_side_effects=True,
                vmem_limit_bytes=64 * 2**20 - 2**18,
            ),
            cost_estimate=pl.CostEstimate(
                flops=3 * 2 * 448 * 7168 * 1152,
                bytes_accessed=4 * 56 * 9216,
                transcendentals=0,
            ),
        )(ortho_in)
        return padded[:rows]

    spec = P(("row", "col"), None)
    return jax.shard_map(
        step, mesh=mesh, in_specs=(spec,), out_specs=spec, check_vma=False
    )
```

```python
import functools
import math

import jax
import jax.numpy as jnp
from jax import lax
from jax.experimental import pallas as pl
from jax.experimental.pallas import tpu as pltpu
from jax.sharding import PartitionSpec as P

coef_a = 3.4445
coef_b = -4.775
coef_c = 2.0315

MESH = pl.DeviceIdType.MESH
F32 = jnp.float32
BF16 = jnp.bfloat16

STEPS = 7
T16 = 16
ROWS = STEPS * T16
HALF = 56
PAD = 64
PW = 1152
SEG = 256
BLK = 4 * SEG
UNIT = BLK // 2
X_PASS = (0, PW, 512)
Y_PASS = ((0, 512, 256), (512, 384, 128), (896, 256, 128))
RELAYED = (2, 4)

ORDER = (
    "a1", "x1o", "a0", "a3", "x0o", "a2", "x1q", "x1p", "x1m", "x2o", "a4", "x0m", "x1r", "x2m",
    "a5", "x3o", "x1b", "x0q", "a6", "g10", "x2p", "x0r", "x2q", "g00", "x2r", "x3q", "x4o", "s10",
    "g20", "x1e", "x2b", "x3p", "x3m", "x3r", "s00", "g11", "x4m", "x0p", "g30", "x2e", "x3b",
    "x4q", "s20", "x5o", "s11", "t00", "x4r", "g21", "x3e", "x0b", "x6o", "g40", "g31", "t10",
    "x5q", "s30", "x0e", "s21", "x4p", "t20", "x5m", "t11", "g01", "x6m", "x5p", "x6q", "x5r",
    "x6p", "w20", "s31", "g50", "s40", "x5b", "t21", "s01", "x4b", "x6r", "g60", "x5e", "x6b",
    "t30", "x4e", "t31", "w10", "s50", "g51", "t01", "x6e", "s60", "g41", "w11", "g61", "t40",
    "t50", "s51", "s41", "w00", "w21", "s61", "w31", "t60", "h1", "t51", "w30", "t41", "w01", "w60",
    "h2", "w50", "t61", "w40", "w51", "w41", "h4", "l0", "h0", "w61", "h6", "i2", "f0", "y00o",
    "y10o", "y20o", "i4", "y00p", "j2", "y10m", "j4", "i1", "y20p", "y20m", "y00q", "y00b", "y20q",
    "i0", "y10p", "y00m", "l1", "y10q", "i6", "f1", "y01o", "j1", "y11o", "y21o", "y10r", "j6",
    "j0", "y00r", "y10b", "k2", "y01p", "y01q", "y01m", "l2", "f2", "k4", "y11q", "y02o", "y20b",
    "y11p", "y01r", "y00e", "y01b", "y11m", "y10e", "y20r", "y21p", "y02m", "y02q", "y02p", "y12o",
    "l3", "f3", "y03o", "z10", "y11b", "z00", "y02r", "y11r", "y12m", "y12p", "y02b", "y03q",
    "y03m", "y03p", "y13o", "y01e", "y20e", "z01", "y12q", "y11e", "y03r", "y22o", "y12r", "y03b",
    "z20", "y12b", "y13p", "y13q", "y21m", "y13m", "y02e", "z11", "y23o", "y21q", "y03e", "y22m",
    "z02", "y22q", "y12e", "y13b", "z03", "y13r", "y23p", "y23q", "y22p", "o0", "y23m", "y21r",
    "y22r", "y21b", "y13e", "z12", "y22b", "y23b", "y23r", "z13", "o1", "y21e", "y22e", "y23e",
    "z21", "z22", "z23", "o2", "v0", "v1", "v2",
)


def kernel(
    inv_square,
    xin,
    out,
    xv,
    xl,
    ain,
    xp,
    yp,
    pbuf,
    rbuf,
    rx,
    gb,
    zacc,
    fin,
    sem_in,
    sem_a2a,
    sem_ag,
    sem_agd,
    sem_rs,
    sem_g,
    sem_back,
    sem_send,
):
    row, col = lax.axis_index("row"), lax.axis_index("col")
    k = row % 2
    y = (row // 2) % 4
    x = (col % 2) * 2 + row // 8
    z = col // 2
    r_x = ((x + 1) // 2) % 2
    c_x = x // 2

    def dev(xx, yy, zz, kk):
        return (((xx % 2) * 4 + yy) * 2 + kk, zz * 2 + xx // 2)

    x_row = x + 1 - 2 * (x % 2)
    x_col = 3 - x
    ring = {1: dev(x, (y + 1) % 4, z, k), -1: dev(x, (y + 3) % 4, z, k)}
    pair = dev(x_row, y, z, k)
    zring = {1: dev(x, y, (z + 1) % 4, k), -1: dev(x, y, (z + 3) % 4, k)}
    cpair = dev(x_col, y, z, k)
    sib = dev(x, y, z, 1 - k)
    same = k == c_x
    other = k + c_x - 2 * k * c_x
    x_far = x + (x_col - x) * other

    def rdma(src, dst, ssem, rsem, device):
        return pltpu.make_async_remote_copy(
            src_ref=src,
            dst_ref=dst,
            send_sem=ssem,
            recv_sem=rsem,
            device_id=device,
            device_id_type=MESH,
        )

    def wait_bytes(ref, sem):
        pltpu.make_async_copy(ref, ref, sem).wait()

    def rows_at(start, n):
        return pl.ds(pl.multiple_of(start, 16), n)

    def cols_at(start, n):
        return pl.ds(pl.multiple_of(start, 128), n)

    def move(src, dst, ssem, rsem, device, self_too):
        if not self_too:
            rdma(src, dst, ssem, rsem, device).start()
            return

        @pl.when(same)
        def _():
            pltpu.make_async_copy(src, dst, rsem).start()

        @pl.when(jnp.logical_not(same))
        def _():
            rdma(src, dst, ssem, rsem, device).start()

    load = pltpu.make_async_copy(xin, xv, sem_in.at[0])
    load.start()

    barrier = pltpu.get_barrier_semaphore()

    def greet(device):
        pl.semaphore_signal(barrier, inc=1, device_id=device, device_id_type=MESH)

    way_in = []
    for d in (0, 1, 3, 2):
        for i in range(2):
            xx, cc = (x, c_x) if i == 0 else (x_col, 1 - c_x)
            zz = (z + d) % 4
            way_in.append((dev(xx, y, zz, c_x), cc, zz, d == 0 and i == 0))
    way_back = []
    for d in (2, 1, 3, 0):
        for i in range(2):
            kk = k if i == 0 else 1 - k
            zz = (z + d) % 4
            way_back.append((dev(x_far, y, zz, kk), zz, kk, d == 0 and i == 0))
    for d in (ring[1], ring[-1], pair, sib):
        greet(d)
    for d, _, _, self_too in way_back:
        if not self_too:
            greet(d)
    back_self = way_back[-2][0]

    @pl.when(jnp.logical_not(same))
    def _():
        greet(back_self)

    pl.semaphore_wait(barrier, 11 + other)

    my_slot = (r_x * 2 + k) * 4 + y

    def slot_rows(slot):
        return rows_at(slot * T16, T16)

    their_slot = slot_rows((r_x * 2 + c_x) * 4 + y)

    def distribute(i):
        for device, cc, zz, self_too in way_in:
            cols = cols_at((cc * 4 + zz) * PW, PW)
            if i < 3:
                src = xin.at[pl.ds(i * T16, T16), cols]
                dst = xp.at[2 * i + k, z, their_slot]
                sem = sem_a2a.at[2 * i + k]
            else:
                src = xl.at[:, cols]
                dst = ain.at[z * 2 + k]
                sem = sem_a2a.at[6]
            move(src, dst, sem_send.at[0, 1 if self_too else 0], sem, device, self_too)

    for i in range(3):
        distribute(i)
    load.wait()
    xl[...] = jnp.concatenate(
        [xv[...].astype(F32)[48:], jnp.zeros((8, 8 * PW), F32)], axis=0
    ).astype(BF16)
    distribute(3)

    def assemble(u):
        if u < 6:
            wait_bytes(xp.at[u, :, slot_rows(my_slot)], sem_a2a.at[u])
            return
        wait_bytes(ain, sem_a2a.at[6])
        for v in range(4):
            xp[6, v, slot_rows(my_slot), :] = jnp.concatenate(
                [ain[v * 2 + kk].astype(F32)[:8] for kk in range(2)], axis=0
            ).astype(BF16)

    class Gather:
        IDX = {
            (0, -1, "AB"): 0,
            (0, 1, "AB"): 1,
            (0, 2, "AB"): 2,
            (1, 0, "AB"): 3,
            (1, -1, "A"): 4,
            (1, -1, "B"): 5,
            (1, 1, "A"): 6,
            (1, 1, "B"): 7,
            (1, 2, "A"): 8,
            (1, 2, "B"): 9,
        }

        def __init__(self, i, par, cols, area, whole):
            self.i, self.par, self.area, self.whole = i, par, area, whole
            self.start, self.width, self.cut = cols

        def piece(self, s, e, part="AB"):
            rr = r_x if s == 0 else 1 - r_x
            slot = (rr * 2 + k) * 4 + (y + e + 4) % 4
            cols = pl.ds(self.start, self.width)
            if part == "A":
                cols = pl.ds(self.start, self.cut)
            elif part == "B":
                cols = pl.ds(self.start + self.cut, self.width - self.cut)
            return self.area(slot_rows(slot), cols)

        def rsem(self, *key):
            return sem_ag.at[self.i, self.IDX[key]]

        def send(self, s, e, part, device, key):
            ref = self.piece(s, e, part)
            rdma(ref, ref, sem_agd.at[self.i, 0], self.rsem(*key), device).start()

        def side(self, s, kk):
            rr = r_x if s == 0 else 1 - r_x
            return self.area(
                rows_at((rr * 2 + kk) * 4 * T16, 4 * T16),
                pl.ds(self.start, self.width),
            )

        def to_sib(self, s):
            ref = self.side(s, k)
            rdma(
                ref, ref, sem_agd.at[self.i, 1], sem_agd.at[self.i, 2 + s], sib
            ).start()

        def wait(self, s, e, part):
            wait_bytes(self.piece(s, e, part), self.rsem(s, e, part))

        def o(self):
            self.send(0, 0, "AB", ring[1], (0, -1, "AB"))
            self.send(0, 0, "AB", ring[-1], (0, 1, "AB"))
            self.send(0, 0, "AB", pair, (1, 0, "AB"))

        def p(self):
            self.wait(1, 0, "AB")
            for s in (self.par, -self.par):
                self.send(1, 0, "B", ring[s], (1, -s, "B"))

        def first(self, e):
            self.wait(0, e, "AB")
            if e == -self.par:
                self.send(0, e, "AB", ring[self.par], (0, 2, "AB"))
            self.send(0, e, "A", pair, (1, e, "A"))

        def m(self):
            self.first(-1)

        def q(self):
            self.first(1)

        def b(self):
            self.wait(1, -self.par, "B")
            self.send(1, -self.par, "B", ring[self.par], (1, 2, "B"))

        def r(self):
            self.wait(0, 2, "AB")
            self.send(0, 2, "A", pair, (1, 2, "A"))
            self.to_sib(0)

        def e(self):
            self.wait(1, self.par, "B")
            for e in (-1, 1):
                self.wait(1, e, "A")
            self.wait(1, 2, "B")
            self.wait(1, 2, "A")
            self.to_sib(1)

        def here(self, s):
            wait_bytes(self.side(s, 1 - k), sem_agd.at[self.i, 2 + s])

        def sent(self):
            cols = pl.ds(self.start, self.width)
            wait_bytes(self.whole(cols), sem_agd.at[self.i, 0])
            wait_bytes(self.area(pl.ds(0, 8 * T16), cols), sem_agd.at[self.i, 1])

    def x_gather(u):
        return Gather(
            u,
            1 - 2 * (u % 2),
            X_PASS,
            lambda rows, cols: xp.at[u, :, rows, cols],
            lambda cols: xp.at[u, :, pl.ds(0, 7 * T16), cols],
        )

    def y_gather(n, t):
        return Gather(
            STEPS + 4 * n + t,
            1 - 2 * (t % 2),
            Y_PASS[n],
            lambda rows, cols: yp.at[:, steps[t], rows, cols],
            lambda cols: yp.at[:, 0, pl.ds(0, 7 * T16), cols],
        )

    steps = [z, (z + 3) % 4, (z + 1) % 4, (z + 2) % 4]
    ax = [x_gather(u) for u in range(STEPS)]
    ay = [[y_gather(n, t) for t in range(4)] for n in range(len(Y_PASS))]

    def side_rows(c):
        rr = r_x if c == 0 else 1 - r_x
        return rows_at(rr * 128, 128)

    def partial_gram(u, c):
        ax[u].here(c)
        tile = jnp.concatenate(
            [
                xp[i, v, slot_rows(my_slot), :]
                for v in range(4)
                for i in range(STEPS)
            ],
            axis=0,
        )
        part = lax.dot_general(
            tile,
            xp[u, :, side_rows(c), :].reshape(UNIT, PW),
            (((1,), (1,)), ((), ())),
            preferred_element_type=F32,
        ).astype(BF16)
        for v in range(4):
            pbuf[u, c, v] = part[v * ROWS : (v + 1) * ROWS]
        s = 1 if c == 0 else -1
        rs_send(pbuf.at[u, c, (z + 2) % 4], rbuf.at[u, c, 0], u, c, 0, zring[s])
        rs_send(pbuf.at[u, c, (z + 4 - s) % 4], rbuf.at[u, c, 1], u, c, 1, zring[-s])

    def rs_send(src, dst, u, c, i, device):
        rdma(src, dst, sem_send.at[1, u], sem_rs.at[u * 2 + c, i], device).start()

    def rs_mid(u, c):
        s = 1 if c == 0 else -1
        v = (z + 4 + s) % 4
        wait_bytes(rbuf.at[u, c, 0], sem_rs.at[u * 2 + c, 0])
        pbuf[u, c, v] = (
            pbuf[u, c, v].astype(F32) + rbuf[u, c, 0].astype(F32)
        ).astype(BF16)
        rs_send(pbuf.at[u, c, v], rbuf.at[u, c, 2], u, c, 2, zring[s])

    def rs_sum(u, c):
        wait_bytes(rbuf.at[u, c, 1], sem_rs.at[u * 2 + c, 1])
        wait_bytes(rbuf.at[u, c, 2], sem_rs.at[u * 2 + c, 2])
        pbuf[u, c, z] = (
            pbuf[u, c, z].astype(F32)
            + rbuf[u, c, 1].astype(F32)
            + rbuf[u, c, 2].astype(F32)
        ).astype(BF16)
        rs_send(pbuf.at[u, c, z], rx.at[u, c], u, c, 3, cpair)

    def rs_end(u, c):
        wait_bytes(rx.at[u, c], sem_rs.at[u * 2 + c, 3])
        total = pbuf[u, c, z].astype(F32) + rx[u, c].astype(F32)
        done = (total * inv_square).astype(BF16)
        rr = r_x if c == 0 else 1 - r_x
        for v in range(4):
            gb[z, u, :, cols_at(v * SEG + rr * 128, 128)] = done[
                :, v * 128 : (v + 1) * 128
            ]

    CLASSES = list(RELAYED) + [
        b for b in range(STEPS) if b not in RELAYED and b - 1 not in RELAYED
    ]

    def g_u(b):
        return b + c_x if b in RELAYED else b

    def gref(e, u, half=None):
        ref = gb.at[(z + e + 4) % 4, u]
        return ref if half is None else ref.at[:, pl.ds(half * UNIT, UNIT)]

    def g_send(ref, device, b, i):
        rdma(ref, ref, sem_send.at[2, 0], sem_g.at[b, i], device).start()

    def g_own(b):
        g_send(gref(0, g_u(b)), zring[1], b, 0)
        g_send(gref(0, g_u(b)), zring[-1], b, 1)

    def g_pass(b, e):
        u = g_u(b)
        half = 0 if e == -1 else 1
        wait_bytes(gref(e, u), sem_g.at[b, half])
        g_send(gref(e, u, half), zring[-e], b, 2 + half)
        if b in RELAYED:
            g_send(gref(e, u), cpair, b, 4 + half)

    def g_far(b):
        for half in range(2):
            wait_bytes(gref(2, g_u(b), half), sem_g.at[b, 2 + half])

    def g_far_pair(b):
        g_far(b)
        g_send(gref(2, g_u(b)), cpair, b, 6)

    def first_prod(t, part):
        e = (0, -1, 1, 2)[t]
        if t > 0 and part == 0:
            for b in RELAYED:
                wait_bytes(gref(e, b + 1 - c_x), sem_g.at[b, 3 + t])
        if t == 3:
            for b in CLASSES:
                if b not in RELAYED and (b == STEPS - 1) == (part == 1):
                    g_far(b)
        v = steps[t]
        acc = zacc.at[pl.ds(t * ROWS, ROWS)]
        for u in range(STEPS - 1) if part == 0 else (STEPS - 1,):
            term = jnp.dot(
                gb[v, u], xp[u].reshape(BLK, PW), preferred_element_type=F32
            )
            if u == 0:
                acc[...] = term
            else:
                acc[...] += term
        if part == 1:
            for i in range(STEPS):
                yp[i, v, slot_rows(my_slot), :] = acc[pl.ds(i * T16, T16), :].astype(
                    BF16
                )

    def second_prod(n, t):
        ay[n][t].here(0)
        ay[n][t].here(1)
        v = steps[t]
        cols = pl.ds(Y_PASS[n][0], Y_PASS[n][1])
        g = jnp.concatenate(
            [
                jnp.concatenate(
                    [gb[j, i, :, cols_at(v * SEG, SEG)] for i in range(STEPS)], axis=1
                )
                for j in range(4)
            ],
            axis=0,
        )
        term = jnp.dot(
            g,
            yp[:, v, :, cols].reshape(STEPS * SEG, Y_PASS[n][1]),
            preferred_element_type=F32,
        )
        if t == 0:
            zacc[:, cols] = term
        else:
            zacc[:, cols] += term

    def combine(n):
        cols = pl.ds(Y_PASS[n][0], Y_PASS[n][1])
        gap = jnp.zeros((PAD - HALF, Y_PASS[n][1]), F32)
        for j in range(0, 8, 2):
            v = way_back[j][1]
            it = [
                coef_a * xp[i, v, slot_rows(my_slot), cols].astype(F32)
                + coef_b * yp[i, v, slot_rows(my_slot), cols].astype(F32)
                + coef_c * zacc[rows_at(v * ROWS + i * T16, T16), cols]
                for i in range(STEPS)
            ]
            for kk in range(2):
                mine = [it[kk], it[kk + 2], it[kk + 4], it[6][kk * 8 : kk * 8 + 8], gap]
                fin[rows_at((v * 2 + kk) * PAD, PAD), cols] = jnp.concatenate(
                    mine, axis=0
                ).astype(BF16)
            for device, zz, kk, self_too in way_back[j : j + 2]:
                move(
                    fin.at[rows_at((zz * 2 + kk) * PAD, PAD), cols],
                    out.at[
                        :, cols_at((c_x * 4 + z) * PW + Y_PASS[n][0], Y_PASS[n][1])
                    ],
                    sem_send.at[3 + n, 1 if self_too else 0],
                    sem_back.at[n, c_x * 4 + z],
                    device,
                    self_too,
                )

    def collect(n):
        start, width, _ = Y_PASS[n]
        for g in range(8):
            ref = fin.at[pl.ds(g * PAD, PAD), pl.ds(start, width)]
            wait_bytes(ref, sem_back.at[n, g])

    for name in [name for name in ORDER if name[0] != "v"]:
        kind, args = name[0], [int(i) for i in name[1:] if i.isdigit()]
        if kind == "x":
            getattr(ax[args[0]], name[-1])()
        elif kind == "y":
            getattr(ay[args[0]][args[1]], name[-1])()
        elif kind in "ij":
            g_pass(args[0], -1 if kind == "i" else 1)
        else:
            {
                "a": assemble,
                "g": partial_gram,
                "s": rs_mid,
                "t": rs_sum,
                "w": rs_end,
                "h": g_own,
                "k": g_far_pair,
                "l": lambda t: first_prod(t, 0),
                "f": lambda t: first_prod(t, 1),
                "z": second_prod,
                "o": combine,
            }[kind](*args)

    for g in (*ax, *(g for n in ay for g in n)):
        g.sent()
    for u in range(STEPS):
        wait_bytes(pbuf.at[u], sem_send.at[1, u])
    wait_bytes(gb.at[pl.ds(0, 3)], sem_send.at[2, 0])
    wait_bytes(yp.at[0, pl.ds(0, 2), pl.ds(0, 7 * 32)], sem_send.at[0, 0])
    for n, (start, width, _) in enumerate(Y_PASS):
        wait_bytes(
            fin.at[pl.ds(0, 7 * PAD), pl.ds(start, width)], sem_send.at[3 + n, 0]
        )

    @pl.when(jnp.logical_not(same))
    def _():
        wait_bytes(yp.at[0, 0, pl.ds(0, PAD)], sem_send.at[0, 1])
        for n, (start, width, _) in enumerate(Y_PASS):
            wait_bytes(
                fin.at[pl.ds(0, PAD), pl.ds(start, width)], sem_send.at[3 + n, 1]
            )

    for n in range(len(Y_PASS)):
        collect(n)


def solution(mesh):
    def step(ortho_in):
        rows, full_cols = ortho_in.shape
        full_rows = rows * mesh.size
        inv_square = 1.0 / (math.sqrt(full_rows) + math.sqrt(full_cols)) ** 2
        vmem = pltpu.VMEM
        dma = pltpu.SemaphoreType.DMA
        n = len(Y_PASS)
        padded = pl.pallas_call(
            functools.partial(kernel, inv_square),
            name="newton_schulz",
            out_shape=jax.ShapeDtypeStruct((PAD, full_cols), BF16),
            in_specs=[pl.BlockSpec(memory_space=pl.ANY)],
            out_specs=pl.BlockSpec(memory_space=pl.ANY),
            scratch_shapes=[
                vmem((HALF, 8 * PW), BF16),
                vmem((T16, 8 * PW), BF16),
                vmem((8, T16, PW), BF16),
                vmem((STEPS, 4, SEG, PW), BF16),
                vmem((STEPS, 4, SEG, PW), BF16),
                vmem((STEPS, 2, 4, ROWS, UNIT), BF16),
                vmem((STEPS, 2, 3, ROWS, UNIT), BF16),
                vmem((STEPS, 2, ROWS, UNIT), BF16),
                vmem((4, STEPS, ROWS, BLK), BF16),
                vmem((4 * ROWS, PW), F32),
                vmem((8 * PAD, PW), BF16),
                dma((1,)),
                dma((STEPS,)),
                dma((STEPS + 4 * n, 10)),
                dma((STEPS + 4 * n, 4)),
                dma((2 * STEPS, 4)),
                dma((STEPS, 7)),
                dma((n, 8)),
                dma((3 + n, 8)),
            ],
            compiler_params=pltpu.CompilerParams(
                collective_id=0,
                has_side_effects=True,
                vmem_limit_bytes=64 * 2**20 - 2**18,
            ),
            cost_estimate=pl.CostEstimate(
                flops=3 * 2 * 448 * 7168 * 1152,
                bytes_accessed=4 * 56 * 9216,
                transcendentals=0,
            ),
        )(ortho_in)
        return padded[:rows]

    spec = P(("row", "col"), None)
    return jax.shard_map(
        step, mesh=mesh, in_specs=(spec,), out_specs=spec, check_vma=False
    )
```

```python
import functools
import math

import jax
import jax.numpy as jnp
from jax import lax
from jax.experimental import pallas as pl
from jax.experimental.pallas import tpu as pltpu
from jax.sharding import PartitionSpec as P

coef_a = 3.4445
coef_b = -4.775
coef_c = 2.0315

MESH = pl.DeviceIdType.MESH
F32 = jnp.float32
BF16 = jnp.bfloat16

STEPS = 7
T16 = 16
ROWS = STEPS * T16
HALF = 56
PAD = 64
PW = 1152
SEG = 256
BLK = 4 * SEG
UNIT = BLK // 2
X_PASS = (0, PW, 512)
Y_PASS = ((0, 512, 256), (512, 384, 128), (896, 256, 128))
RELAYED = (2, 4)

ORDER = (
    "a1", "x1o", "a0", "a3", "x0o", "a2", "x1q", "x1p", "x1m", "x2o", "a4", "x0m", "x1r", "x2m",
    "a5", "x3o", "x1b", "x0q", "a6", "g10", "x2p", "x0r", "x2q", "g00", "x2r", "x3q", "x4o", "s10",
    "x1e", "g20", "x2b", "x3p", "x3m", "x3r", "s00", "g11", "x4m", "x0p", "g30", "x2e", "x3b",
    "x4q", "s20", "x5o", "s11", "t00", "x4r", "g21", "x3e", "x0b", "x6o", "g40", "s30", "g31",
    "t10", "x5q", "x0e", "s21", "x4p", "t20", "x5m", "t11", "g01", "x6m", "x5p", "x6q", "x5r",
    "x6p", "x4b", "w20", "s31", "g50", "s40", "x5b", "t21", "s01", "x6r", "g60", "x5e", "x6b",
    "t30", "x4e", "t31", "w10", "s50", "g51", "t01", "x6e", "s60", "g41", "w11", "g61", "t40",
    "s51", "w31", "w00", "t50", "w21", "s41", "s61", "t60", "h1", "w40", "t51", "t41", "w30", "h2",
    "w50", "w01", "w60", "t61", "w51", "w41", "h4", "l0", "h0", "w61", "h6", "i2", "f0", "y00o",
    "y10o", "y20o", "i4", "y00p", "j2", "y10m", "j4", "i1", "y20p", "y20m", "y00q", "y00b", "y20q",
    "i0", "y10p", "y00m", "l1", "y10q", "i6", "f1", "y01o", "j1", "y11o", "y21o", "y10r", "j6",
    "y00r", "y10b", "k2", "y01p", "y01q", "j0", "y01m", "l2", "f2", "k4", "y11q", "y02o", "y11p",
    "y01r", "y00e", "y01b", "y11m", "y10e", "y20b", "y20r", "y21p", "y02m", "y02q", "y02p", "y12o",
    "l3", "f3", "y03o", "z10", "y11b", "z00", "y02r", "y11r", "y12p", "y12m", "y02b", "y03q",
    "y03m", "y03p", "y13o", "y01e", "y20e", "z01", "y12q", "y11e", "y03r", "y22o", "y12r", "y03b",
    "z20", "y12b", "y13p", "y13q", "y21m", "y13m", "y02e", "z11", "y23o", "y21q", "y03e", "y22m",
    "z02", "y22q", "y12e", "y13b", "z03", "y13r", "y23p", "y23q", "y22p", "o0", "y23m", "y21r",
    "y22r", "y21b", "y13e", "z12", "y22b", "y23b", "y23r", "z13", "o1", "y21e", "y22e", "y23e",
    "z21", "z22", "z23", "o2", "v0", "v1", "v2",
)


def kernel(
    inv_square,
    xin,
    out,
    xv,
    xl,
    ain,
    xp,
    yp,
    pbuf,
    rbuf,
    rx,
    gb,
    zacc,
    fin,
    sem_in,
    sem_a2a,
    sem_ag,
    sem_agd,
    sem_rs,
    sem_g,
    sem_back,
    sem_send,
):
    row, col = lax.axis_index("row"), lax.axis_index("col")
    k = row % 2
    y = (row // 2) % 4
    x = (col % 2) * 2 + row // 8
    z = col // 2
    r_x = ((x + 1) // 2) % 2
    c_x = x // 2

    def dev(xx, yy, zz, kk):
        return (((xx % 2) * 4 + yy) * 2 + kk, zz * 2 + xx // 2)

    x_row = x + 1 - 2 * (x % 2)
    x_col = 3 - x
    ring = {1: dev(x, (y + 1) % 4, z, k), -1: dev(x, (y + 3) % 4, z, k)}
    pair = dev(x_row, y, z, k)
    zring = {1: dev(x, y, (z + 1) % 4, k), -1: dev(x, y, (z + 3) % 4, k)}
    cpair = dev(x_col, y, z, k)
    sib = dev(x, y, z, 1 - k)
    same = k == c_x
    other = k + c_x - 2 * k * c_x
    x_far = x + (x_col - x) * other

    def rdma(src, dst, ssem, rsem, device):
        return pltpu.make_async_remote_copy(
            src_ref=src,
            dst_ref=dst,
            send_sem=ssem,
            recv_sem=rsem,
            device_id=device,
            device_id_type=MESH,
        )

    def wait_bytes(ref, sem):
        pltpu.make_async_copy(ref, ref, sem).wait()

    def rows_at(start, n):
        return pl.ds(pl.multiple_of(start, 16), n)

    def cols_at(start, n):
        return pl.ds(pl.multiple_of(start, 128), n)

    def move(src, dst, ssem, rsem, device, self_too):
        if not self_too:
            rdma(src, dst, ssem, rsem, device).start()
            return

        @pl.when(same)
        def _():
            pltpu.make_async_copy(src, dst, rsem).start()

        @pl.when(jnp.logical_not(same))
        def _():
            rdma(src, dst, ssem, rsem, device).start()

    load = pltpu.make_async_copy(xin, xv, sem_in.at[0])
    load.start()

    barrier = pltpu.get_barrier_semaphore()

    def greet(device):
        pl.semaphore_signal(barrier, inc=1, device_id=device, device_id_type=MESH)

    way_in = []
    for d in (0, 1, 3, 2):
        for i in range(2):
            xx, cc = (x, c_x) if i == 0 else (x_col, 1 - c_x)
            zz = (z + d) % 4
            way_in.append((dev(xx, y, zz, c_x), cc, zz, d == 0 and i == 0))
    way_back = []
    for d in (2, 1, 3, 0):
        for i in range(2):
            kk = k if i == 0 else 1 - k
            zz = (z + d) % 4
            way_back.append((dev(x_far, y, zz, kk), zz, kk, d == 0 and i == 0))
    for d in (ring[1], ring[-1], pair, sib):
        greet(d)
    for d, _, _, self_too in way_back:
        if not self_too:
            greet(d)
    back_self = way_back[-2][0]

    @pl.when(jnp.logical_not(same))
    def _():
        greet(back_self)

    pl.semaphore_wait(barrier, 11 + other)

    my_slot = (r_x * 2 + k) * 4 + y

    def slot_rows(slot):
        return rows_at(slot * T16, T16)

    their_slot = slot_rows((r_x * 2 + c_x) * 4 + y)

    def distribute(i):
        for device, cc, zz, self_too in way_in:
            cols = cols_at((cc * 4 + zz) * PW, PW)
            if i < 3:
                src = xin.at[pl.ds(i * T16, T16), cols]
                dst = xp.at[2 * i + k, z, their_slot]
                sem = sem_a2a.at[2 * i + k]
            else:
                src = xl.at[:, cols]
                dst = ain.at[z * 2 + k]
                sem = sem_a2a.at[6]
            move(src, dst, sem_send.at[0, 1 if self_too else 0], sem, device, self_too)

    for i in range(3):
        distribute(i)
    load.wait()
    xl[...] = jnp.concatenate(
        [xv[...].astype(F32)[48:], jnp.zeros((8, 8 * PW), F32)], axis=0
    ).astype(BF16)
    distribute(3)

    def assemble(u):
        if u < 6:
            wait_bytes(xp.at[u, :, slot_rows(my_slot)], sem_a2a.at[u])
            return
        wait_bytes(ain, sem_a2a.at[6])
        for v in range(4):
            xp[6, v, slot_rows(my_slot), :] = jnp.concatenate(
                [ain[v * 2 + kk].astype(F32)[:8] for kk in range(2)], axis=0
            ).astype(BF16)

    class Gather:
        IDX = {
            (0, -1, "AB"): 0,
            (0, 1, "AB"): 1,
            (0, 2, "AB"): 2,
            (1, 0, "AB"): 3,
            (1, -1, "A"): 4,
            (1, -1, "B"): 5,
            (1, 1, "A"): 6,
            (1, 1, "B"): 7,
            (1, 2, "A"): 8,
            (1, 2, "B"): 9,
        }

        def __init__(self, i, par, cols, area, whole):
            self.i, self.par, self.area, self.whole = i, par, area, whole
            self.start, self.width, self.cut = cols

        def piece(self, s, e, part="AB"):
            rr = r_x if s == 0 else 1 - r_x
            slot = (rr * 2 + k) * 4 + (y + e + 4) % 4
            cols = pl.ds(self.start, self.width)
            if part == "A":
                cols = pl.ds(self.start, self.cut)
            elif part == "B":
                cols = pl.ds(self.start + self.cut, self.width - self.cut)
            return self.area(slot_rows(slot), cols)

        def rsem(self, *key):
            return sem_ag.at[self.i, self.IDX[key]]

        def send(self, s, e, part, device, key):
            ref = self.piece(s, e, part)
            rdma(ref, ref, sem_agd.at[self.i, 0], self.rsem(*key), device).start()

        def side(self, s, kk):
            rr = r_x if s == 0 else 1 - r_x
            return self.area(
                rows_at((rr * 2 + kk) * 4 * T16, 4 * T16),
                pl.ds(self.start, self.width),
            )

        def to_sib(self, s):
            ref = self.side(s, k)
            rdma(
                ref, ref, sem_agd.at[self.i, 1], sem_agd.at[self.i, 2 + s], sib
            ).start()

        def wait(self, s, e, part):
            wait_bytes(self.piece(s, e, part), self.rsem(s, e, part))

        def o(self):
            self.send(0, 0, "AB", ring[1], (0, -1, "AB"))
            self.send(0, 0, "AB", ring[-1], (0, 1, "AB"))
            self.send(0, 0, "AB", pair, (1, 0, "AB"))

        def p(self):
            self.wait(1, 0, "AB")
            for s in (self.par, -self.par):
                self.send(1, 0, "B", ring[s], (1, -s, "B"))

        def first(self, e):
            self.wait(0, e, "AB")
            if e == -self.par:
                self.send(0, e, "AB", ring[self.par], (0, 2, "AB"))
            self.send(0, e, "A", pair, (1, e, "A"))

        def m(self):
            self.first(-1)

        def q(self):
            self.first(1)

        def b(self):
            self.wait(1, -self.par, "B")
            self.send(1, -self.par, "B", ring[self.par], (1, 2, "B"))

        def r(self):
            self.wait(0, 2, "AB")
            self.send(0, 2, "A", pair, (1, 2, "A"))
            self.to_sib(0)

        def e(self):
            self.wait(1, self.par, "B")
            for e in (-1, 1):
                self.wait(1, e, "A")
            self.wait(1, 2, "B")
            self.wait(1, 2, "A")
            self.to_sib(1)

        def here(self, s):
            wait_bytes(self.side(s, 1 - k), sem_agd.at[self.i, 2 + s])

        def sent(self):
            cols = pl.ds(self.start, self.width)
            wait_bytes(self.whole(cols), sem_agd.at[self.i, 0])
            wait_bytes(self.area(pl.ds(0, 8 * T16), cols), sem_agd.at[self.i, 1])

    def x_gather(u):
        return Gather(
            u,
            1 - 2 * (u % 2),
            X_PASS,
            lambda rows, cols: xp.at[u, :, rows, cols],
            lambda cols: xp.at[u, :, pl.ds(0, 7 * T16), cols],
        )

    def y_gather(n, t):
        return Gather(
            STEPS + 4 * n + t,
            1 - 2 * (t % 2),
            Y_PASS[n],
            lambda rows, cols: yp.at[:, steps[t], rows, cols],
            lambda cols: yp.at[:, 0, pl.ds(0, 7 * T16), cols],
        )

    steps = [z, (z + 3) % 4, (z + 1) % 4, (z + 2) % 4]
    ax = [x_gather(u) for u in range(STEPS)]
    ay = [[y_gather(n, t) for t in range(4)] for n in range(len(Y_PASS))]

    def side_rows(c):
        rr = r_x if c == 0 else 1 - r_x
        return rows_at(rr * 128, 128)

    def partial_gram(u, c):
        ax[u].here(c)
        tile = jnp.concatenate(
            [
                xp[i, v, slot_rows(my_slot), :]
                for v in range(4)
                for i in range(STEPS)
            ],
            axis=0,
        )
        part = lax.dot_general(
            tile,
            xp[u, :, side_rows(c), :].reshape(UNIT, PW),
            (((1,), (1,)), ((), ())),
            preferred_element_type=F32,
        ).astype(BF16)
        for v in range(4):
            pbuf[u, c, v] = part[v * ROWS : (v + 1) * ROWS]
        s = 1 if c == 0 else -1
        rs_send(pbuf.at[u, c, (z + 2) % 4], rbuf.at[u, c, 0], u, c, 0, zring[s])
        rs_send(pbuf.at[u, c, (z + 4 - s) % 4], rbuf.at[u, c, 1], u, c, 1, zring[-s])

    def rs_send(src, dst, u, c, i, device):
        rdma(src, dst, sem_send.at[1, u], sem_rs.at[u * 2 + c, i], device).start()

    def rs_mid(u, c):
        s = 1 if c == 0 else -1
        v = (z + 4 + s) % 4
        wait_bytes(rbuf.at[u, c, 0], sem_rs.at[u * 2 + c, 0])
        pbuf[u, c, v] = (
            pbuf[u, c, v].astype(F32) + rbuf[u, c, 0].astype(F32)
        ).astype(BF16)
        rs_send(pbuf.at[u, c, v], rbuf.at[u, c, 2], u, c, 2, zring[s])

    def rs_sum(u, c):
        wait_bytes(rbuf.at[u, c, 1], sem_rs.at[u * 2 + c, 1])
        wait_bytes(rbuf.at[u, c, 2], sem_rs.at[u * 2 + c, 2])
        pbuf[u, c, z] = (
            pbuf[u, c, z].astype(F32)
            + rbuf[u, c, 1].astype(F32)
            + rbuf[u, c, 2].astype(F32)
        ).astype(BF16)
        rs_send(pbuf.at[u, c, z], rx.at[u, c], u, c, 3, cpair)

    def rs_end(u, c):
        wait_bytes(rx.at[u, c], sem_rs.at[u * 2 + c, 3])
        total = pbuf[u, c, z].astype(F32) + rx[u, c].astype(F32)
        done = (total * inv_square).astype(BF16)
        rr = r_x if c == 0 else 1 - r_x
        for v in range(4):
            gb[z, u, :, cols_at(v * SEG + rr * 128, 128)] = done[
                :, v * 128 : (v + 1) * 128
            ]

    CLASSES = list(RELAYED) + [
        b for b in range(STEPS) if b not in RELAYED and b - 1 not in RELAYED
    ]

    def g_u(b):
        return b + c_x if b in RELAYED else b

    def gref(e, u, half=None):
        ref = gb.at[(z + e + 4) % 4, u]
        return ref if half is None else ref.at[:, pl.ds(half * UNIT, UNIT)]

    def g_send(ref, device, b, i):
        rdma(ref, ref, sem_send.at[2, 0], sem_g.at[b, i], device).start()

    def g_own(b):
        g_send(gref(0, g_u(b)), zring[1], b, 0)
        g_send(gref(0, g_u(b)), zring[-1], b, 1)

    def g_pass(b, e):
        u = g_u(b)
        half = 0 if e == -1 else 1
        wait_bytes(gref(e, u), sem_g.at[b, half])
        g_send(gref(e, u, half), zring[-e], b, 2 + half)
        if b in RELAYED:
            g_send(gref(e, u), cpair, b, 4 + half)

    def g_far(b):
        for half in range(2):
            wait_bytes(gref(2, g_u(b), half), sem_g.at[b, 2 + half])

    def g_far_pair(b):
        g_far(b)
        g_send(gref(2, g_u(b)), cpair, b, 6)

    def first_prod(t, part):
        e = (0, -1, 1, 2)[t]
        if t > 0 and part == 0:
            for b in RELAYED:
                wait_bytes(gref(e, b + 1 - c_x), sem_g.at[b, 3 + t])
        if t == 3:
            for b in CLASSES:
                if b not in RELAYED and (b == STEPS - 1) == (part == 1):
                    g_far(b)
        v = steps[t]
        acc = zacc.at[pl.ds(t * ROWS, ROWS)]
        for u in range(STEPS - 1) if part == 0 else (STEPS - 1,):
            term = jnp.dot(
                gb[v, u], xp[u].reshape(BLK, PW), preferred_element_type=F32
            )
            if u == 0:
                acc[...] = term
            else:
                acc[...] += term
        if part == 1:
            for i in range(STEPS):
                yp[i, v, slot_rows(my_slot), :] = acc[pl.ds(i * T16, T16), :].astype(
                    BF16
                )

    def second_prod(n, t):
        ay[n][t].here(0)
        ay[n][t].here(1)
        v = steps[t]
        cols = pl.ds(Y_PASS[n][0], Y_PASS[n][1])
        g = jnp.concatenate(
            [
                jnp.concatenate(
                    [gb[j, i, :, cols_at(v * SEG, SEG)] for i in range(STEPS)], axis=1
                )
                for j in range(4)
            ],
            axis=0,
        )
        term = jnp.dot(
            g,
            yp[:, v, :, cols].reshape(STEPS * SEG, Y_PASS[n][1]),
            preferred_element_type=F32,
        )
        if t == 0:
            zacc[:, cols] = term
        else:
            zacc[:, cols] += term

    def combine(n):
        cols = pl.ds(Y_PASS[n][0], Y_PASS[n][1])
        gap = jnp.zeros((PAD - HALF, Y_PASS[n][1]), F32)
        for j in range(0, 8, 2):
            v = way_back[j][1]
            it = [
                coef_a * xp[i, v, slot_rows(my_slot), cols].astype(F32)
                + coef_b * yp[i, v, slot_rows(my_slot), cols].astype(F32)
                + coef_c * zacc[rows_at(v * ROWS + i * T16, T16), cols]
                for i in range(STEPS)
            ]
            for kk in range(2):
                mine = [it[kk], it[kk + 2], it[kk + 4], it[6][kk * 8 : kk * 8 + 8], gap]
                fin[rows_at((v * 2 + kk) * PAD, PAD), cols] = jnp.concatenate(
                    mine, axis=0
                ).astype(BF16)
            for device, zz, kk, self_too in way_back[j : j + 2]:
                move(
                    fin.at[rows_at((zz * 2 + kk) * PAD, PAD), cols],
                    out.at[
                        :, cols_at((c_x * 4 + z) * PW + Y_PASS[n][0], Y_PASS[n][1])
                    ],
                    sem_send.at[3 + n, 1 if self_too else 0],
                    sem_back.at[n, c_x * 4 + z],
                    device,
                    self_too,
                )

    def collect(n):
        start, width, _ = Y_PASS[n]
        for g in range(8):
            ref = fin.at[pl.ds(g * PAD, PAD), pl.ds(start, width)]
            wait_bytes(ref, sem_back.at[n, g])

    for name in [name for name in ORDER if name[0] != "v"]:
        kind, args = name[0], [int(i) for i in name[1:] if i.isdigit()]
        if kind == "x":
            getattr(ax[args[0]], name[-1])()
        elif kind == "y":
            getattr(ay[args[0]][args[1]], name[-1])()
        elif kind in "ij":
            g_pass(args[0], -1 if kind == "i" else 1)
        else:
            {
                "a": assemble,
                "g": partial_gram,
                "s": rs_mid,
                "t": rs_sum,
                "w": rs_end,
                "h": g_own,
                "k": g_far_pair,
                "l": lambda t: first_prod(t, 0),
                "f": lambda t: first_prod(t, 1),
                "z": second_prod,
                "o": combine,
            }[kind](*args)

    for g in (*ax, *(g for n in ay for g in n)):
        g.sent()
    for u in range(STEPS):
        wait_bytes(pbuf.at[u], sem_send.at[1, u])
    wait_bytes(gb.at[pl.ds(0, 3)], sem_send.at[2, 0])
    wait_bytes(yp.at[0, pl.ds(0, 2), pl.ds(0, 7 * 32)], sem_send.at[0, 0])
    for n, (start, width, _) in enumerate(Y_PASS):
        wait_bytes(
            fin.at[pl.ds(0, 7 * PAD), pl.ds(start, width)], sem_send.at[3 + n, 0]
        )

    @pl.when(jnp.logical_not(same))
    def _():
        wait_bytes(yp.at[0, 0, pl.ds(0, PAD)], sem_send.at[0, 1])
        for n, (start, width, _) in enumerate(Y_PASS):
            wait_bytes(
                fin.at[pl.ds(0, PAD), pl.ds(start, width)], sem_send.at[3 + n, 1]
            )

    for n in range(len(Y_PASS)):
        collect(n)


def solution(mesh):
    def step(ortho_in):
        rows, full_cols = ortho_in.shape
        full_rows = rows * mesh.size
        inv_square = 1.0 / (math.sqrt(full_rows) + math.sqrt(full_cols)) ** 2
        vmem = pltpu.VMEM
        dma = pltpu.SemaphoreType.DMA
        n = len(Y_PASS)
        padded = pl.pallas_call(
            functools.partial(kernel, inv_square),
            name="newton_schulz",
            out_shape=jax.ShapeDtypeStruct((PAD, full_cols), BF16),
            in_specs=[pl.BlockSpec(memory_space=pl.ANY)],
            out_specs=pl.BlockSpec(memory_space=pl.ANY),
            scratch_shapes=[
                vmem((HALF, 8 * PW), BF16),
                vmem((T16, 8 * PW), BF16),
                vmem((8, T16, PW), BF16),
                vmem((STEPS, 4, SEG, PW), BF16),
                vmem((STEPS, 4, SEG, PW), BF16),
                vmem((STEPS, 2, 4, ROWS, UNIT), BF16),
                vmem((STEPS, 2, 3, ROWS, UNIT), BF16),
                vmem((STEPS, 2, ROWS, UNIT), BF16),
                vmem((4, STEPS, ROWS, BLK), BF16),
                vmem((4 * ROWS, PW), F32),
                vmem((8 * PAD, PW), BF16),
                dma((1,)),
                dma((STEPS,)),
                dma((STEPS + 4 * n, 10)),
                dma((STEPS + 4 * n, 4)),
                dma((2 * STEPS, 4)),
                dma((STEPS, 7)),
                dma((n, 8)),
                dma((3 + n, 8)),
            ],
            compiler_params=pltpu.CompilerParams(
                collective_id=0,
                has_side_effects=True,
                vmem_limit_bytes=64 * 2**20 - 2**18,
            ),
            cost_estimate=pl.CostEstimate(
                flops=3 * 2 * 448 * 7168 * 1152,
                bytes_accessed=4 * 56 * 9216,
                transcendentals=0,
            ),
        )(ortho_in)
        return padded[:rows]

    spec = P(("row", "col"), None)
    return jax.shard_map(
        step, mesh=mesh, in_specs=(spec,), out_specs=spec, check_vma=False
    )
```
